128 devices in a mesh: wide: 32 (over y, z, x_lo), narrow: 4 (over x_hi, core).
Axes of the slice: x: 4 (x_hi: 2, x_lo: 2; x = x_hi * 2 + x_lo), y: 4, z: 4, core: 2. Of those that a mesh axis runs over, the one named last changes fastest.
Arguments:
- target_hidden: bfloat16 [512, 16384], P(('wide', 'narrow'))
- target_weight: bfloat16 [16384, 65536], P(None, ('wide', 'narrow')), may hold values from -0.046875 to 0.046875
- draft_hidden: bfloat16 [512, 4096], P(('wide', 'narrow'))
- draft_weight: bfloat16 [4096, 65536], P(None, ('wide', 'narrow')), may hold values from -0.09375 to 0.09375
- draft_tokens: int32 [512], replicated, may hold values from 0 to 65535
Outputs:
- target_logprob: float32 [512, 65536], P(None, ('wide', 'narrow'))
- draft_logprob: float32 [512, 65536], P(None, ('wide', 'narrow'))
- residual: float32 [512, 65536], P(None, ('wide', 'narrow'))
- acceptance: float32 [512], replicated
- leftover: float32 [512], replicated
The draws below stay inside these ranges and needn't reach their ends.
All inputs are finite; a program needn't handle non-finite values.
Results may differ from the reference program's by a relative error of at most 0.0011.
Values may be sent and summed in bfloat16 or wider, within the bound.
A program may use at most 128 MiB of HBM per device.

```python
import math
import jax
import jax.numpy as jnp

H = 16384
D = 4096
ROWS = 512
VOCAB = 65536


def row_spread(key, upper):
    unit = jax.random.uniform(jax.random.fold_in(key, 77), (ROWS,), jnp.float32)
    return jnp.exp(math.log(0.1) + unit * math.log(upper / 0.1))


def draw_target_hidden(key, part):
    scales = row_spread(key, 4.0)
    key = jax.random.fold_in(key, 1)
    values = jax.random.normal(key, (ROWS, H), jnp.float32)
    return (values * scales[:, None]).astype(jnp.bfloat16)


def draw_draft_hidden(key, part):
    scales = row_spread(key, 4.0)
    key = jax.random.fold_in(key, 2)
    values = jax.random.normal(key, (ROWS, D), jnp.float32)
    return (values * scales[:, None]).astype(jnp.bfloat16)


def place_ends(entries, rng, low, high):
    spot = [jax.random.randint(jax.random.fold_in(rng, axis), (), 0, length) for axis, length in enumerate(entries.shape)]
    widest = entries.shape.index(max(entries.shape))
    neighbour = spot[:widest] + [(spot[widest] + 1) % entries.shape[widest]] + spot[widest + 1:]
    return entries.at[tuple(spot)].set(low).at[tuple(neighbour)].set(high)


def steps_of(stream_key, dims, pieces, least, largest):
    def one(position, blocks):
        steps = jax.random.uniform(jax.random.fold_in(jax.random.fold_in(stream_key, 6), position), (blocks,), jnp.float32, least / len(pieces), largest / len(pieces))
        return jnp.repeat(jnp.exp(steps), dims[position] // blocks).reshape((-1,) + (1,) * (len(dims) - position - 1))

    factor_of = one(*pieces[0])
    for cut in pieces[1:]:
        factor_of = factor_of * one(*cut)
    return factor_of


def noise(key, shape, scale, limit, shards=(), held_as=jnp.bfloat16):
    values = scale * jax.random.normal(key, shape, jnp.float32)
    if shards:
        values = values * steps_of(key, shape, shards, -0.22, 0.18)
    return jnp.clip(values, -limit, limit).astype(held_as)


def setup_inputs(seed: int = 0) -> dict:
    splits = jax.random.split(jax.random.key(seed), 6)
    return {
        "target_hidden": draw_target_hidden(jax.random.fold_in(splits[5], 71), 0),
        "target_weight": noise(splits[1], (H, VOCAB), H ** -0.5, 0.046875, ((1, 128),)),
        "draft_hidden": draw_draft_hidden(jax.random.fold_in(splits[5], 71), 0),
        "draft_weight": noise(splits[3], (D, VOCAB), D ** -0.5, 0.09375, ((1, 128),)),
        "draft_tokens": place_ends(jax.random.randint(splits[4], (ROWS,), 0, VOCAB), jax.random.fold_in(splits[4], 1), 0, VOCAB - 1).astype(jnp.int32),
    }


def log_probs(logits):
    top = jnp.max(logits, axis=1, keepdims=True)
    total = jnp.sum(jnp.exp(logits - top), axis=1, keepdims=True)
    return logits - (top + jnp.log(total))


def reference(target_hidden, target_weight, draft_hidden, draft_weight, draft_tokens):
    target_logits = jnp.dot(target_hidden, target_weight, preferred_element_type=jnp.float32)
    draft_logits = jnp.dot(draft_hidden, draft_weight, preferred_element_type=jnp.float32)
    target_logprob = log_probs(target_logits)
    draft_logprob = log_probs(draft_logits)
    excess = jnp.maximum(jnp.exp(target_logprob) - jnp.exp(draft_logprob), 0.0)
    leftover = jnp.sum(excess, axis=1)
    residual = excess / jnp.maximum(leftover, 0.25)[:, None]
    chosen = draft_tokens.astype(jnp.int32)[:, None]
    target_pick = jnp.take_along_axis(target_logprob, chosen, axis=1)[:, 0]
    draft_pick = jnp.take_along_axis(draft_logprob, chosen, axis=1)[:, 0]
    acceptance = jnp.exp(jnp.minimum(0.0, target_pick - draft_pick))
    return target_logprob, draft_logprob, residual, acceptance, leftover
```

```python
import functools

import jax
import jax.numpy as jnp
from jax import lax
from jax.experimental import pallas as pl
from jax.experimental.pallas import tpu as pltpu
from jax.sharding import PartitionSpec as P

MESH = pl.DeviceIdType.MESH
T = 128
ORDERS = (("x", "y", "z"), ("y", "z", "x"), ("z", "x", "y"))
SPLIT = (("d", (3, 3, 2)), ("t", (4, 4, 5)), ("t", (4, 4, 4)), ("t", (2, 2, 3)))


def make_units():
    units, used = [], {"d": 0, "t": 0}
    for kind, sizes in SPLIT:
        for order, size in enumerate(sizes):
            units.append((order, kind, used[kind] * T, size * T))
            used[kind] += size
    return units


UNITS = make_units()
GROUPS = len(SPLIT)


def view(sel):
    whole = slice(None)
    x = sel["x"]
    if x == "all":
        hi, lo = whole, whole
    elif isinstance(x, tuple):
        hi, lo = x[1], whole
    else:
        hi, lo = lax.div(x, 2), lax.rem(x, 2)
    rest = []
    for name in ("y", "z"):
        v = sel[name]
        if isinstance(v, str):
            rest.append(whole)
        elif isinstance(v, tuple):
            rest.append(pl.ds(2 * v[1], 2))
        else:
            rest.append(v)
    return (hi, rest[0], rest[1], lo)


def kernel(ht_ref, wt_ref, hd_ref, wd_ref, tok_ref, lt_ref, ld_ref, stat_ref, *scratch):
    n_units = len(UNITS)
    hb = scratch[:n_units]
    wb = scratch[n_units : 2 * n_units]
    (stage_t, stage_d, acc_t, acc_d, part_t, part_d, tok_f, near, far,
     gs, gr, wl, ws, wr, es, er, el, ps, pr, ns, nr, fs, fr, osem) = scratch[2 * n_units :]
    w, n = lax.axis_index("wide"), lax.axis_index("narrow")
    pos = {"x": lax.div(n, 2) * 2 + lax.rem(w, 2), "y": lax.div(w, 8), "z": lax.rem(lax.div(w, 2), 4)}
    c = lax.rem(n, 2)

    def device(dx=0, dy=0, dz=0, dc=0):
        x = lax.rem(pos["x"] + dx, 4)
        y = lax.rem(pos["y"] + dy, 4)
        z = lax.rem(pos["z"] + dz, 4)
        return ((y * 4 + z) * 2 + lax.rem(x, 2), lax.div(x, 2) * 2 + lax.rem(c + dc, 2))

    def shift(dim, by):
        return device(**{"d" + dim: by})

    def remote(src, dst, send, recv, to):
        return pltpu.make_async_remote_copy(
            src_ref=src, dst_ref=dst, send_sem=send, recv_sem=recv, device_id=to, device_id_type=MESH
        )

    partner = device(dc=1)

    local = []
    for u, (order, kind, start, size) in enumerate(UNITS):
        ref = wt_ref if kind == "t" else wd_ref
        local.append(pltpu.make_async_copy(ref.at[c, :, pl.ds(start, size), :], wb[u].at[0], wl.at[u]))
        local[-1].start()
    own_t = pltpu.make_async_copy(
        ht_ref.at[:, pl.ds(pl.multiple_of(c * 8192 + lax.div(n, 2) * 4096, T), 4096)], stage_t.at[n], el.at[0])
    own_d = pltpu.make_async_copy(
        hd_ref.at[:, pl.ds(pl.multiple_of(c * 2048 + lax.div(n, 2) * 1024, T), 1024)], stage_d.at[n], el.at[1])
    own_t.start()
    own_d.start()

    near_offs = [(a, b) for a in range(4) for b in range(2) if (a, b) != (0, 0)]
    far_offs = [(a, b) for a in range(4) for b in range(4) if (a, b) != (0, 0)]
    barrier = pltpu.get_barrier_semaphore()
    for a, b in near_offs:
        pl.semaphore_signal(barrier, inc=1, device_id=device(dx=a, dc=b), device_id_type=MESH)
    for a, b in far_offs:
        pl.semaphore_signal(barrier, inc=1, device_id=device(dy=a, dz=b), device_id_type=MESH)
    pl.semaphore_wait(barrier, len(near_offs) + len(far_offs))

    swaps = []
    for j in range(1, 4):
        to = lax.rem(n + j, 4)
        frm = lax.rem(n + 4 - j, 4)
        qt = pl.multiple_of(lax.rem(to, 2) * 8192 + lax.div(to, 2) * 4096, T)
        qd = pl.multiple_of(lax.rem(to, 2) * 2048 + lax.div(to, 2) * 1024, T)
        send_d = remote(hd_ref.at[:, pl.ds(qd, 1024)], stage_d.at[n], es.at[1, j], er.at[1, j], (w, to))
        send_t = remote(ht_ref.at[:, pl.ds(qt, 4096)], stage_t.at[n], es.at[0, j], er.at[0, j], (w, to))
        send_d.start()
        send_t.start()
        swaps.append(send_d)
        swaps.append(send_t)
    lent = []
    for u, (order, kind, start, size) in enumerate(UNITS):
        ref = wt_ref if kind == "t" else wd_ref
        lent.append(remote(ref.at[1 - c, :, pl.ds(start, size), :], wb[u].at[1], ws.at[u], wr.at[u], partner))
        lent[-1].start()
    own_t.wait()
    own_d.wait()
    for s in swaps:
        s.wait_recv()

    sends = []

    def send(u, k, src, to):
        copy = remote(src, src, gs.at[u, k], gr.at[u, k], to)
        copy.start()
        sends.append(copy)
        return copy

    arriving = {}
    xh, xl = lax.div(pos["x"], 2), lax.rem(pos["x"], 2)

    def line(order, c2, part="all"):
        d1, d2, d3 = order
        return view({d1: part, d2: c2, d3: pos[d3]})

    def plane(order, c3, part="all"):
        d1, d2, d3 = order
        return view({d1: "all", d2: part, d3: c3})

    def up(dim):
        return lax.rem(pos[dim] + 1, 4)

    def down(dim):
        return lax.rem(pos[dim] + 3, 4)

    def phase1(u):
        o, kind, start, size = UNITS[u]
        order = ORDERS[o]
        stage = stage_t if kind == "t" else stage_d
        rows = [stage[j, :, start : start + size].astype(jnp.float32) for j in range(4)]
        hb[u][xh, pos["y"], pos["z"], xl] = jnp.concatenate(rows, axis=0).astype(jnp.bfloat16)
        mine = hb[u].at[xh, pos["y"], pos["z"], xl]
        arriving[u, 1] = [send(u, k, mine, shift(order[0], by)) for k, by in ((0, 1), (1, 3), (2, 2))]

    def arrived(u, phase):
        for copy in arriving[u, phase]:
            copy.wait_recv()

    def phase2a(u):
        order = ORDERS[UNITS[u][0]]
        arrived(u, 1)
        mine = hb[u].at[line(order, pos[order[1]])]
        arriving[u, 2] = [send(u, k, mine, shift(order[1], by)) for k, by in ((3, 1), (4, 3))]

    def phase2b(u):
        order = ORDERS[UNITS[u][0]]
        arrived(u, 2)
        d = order[1]
        arriving[u, 3] = [
            send(u, 5, hb[u].at[line(order, down(d), ("half", 0))], shift(d, 1)),
            send(u, 6, hb[u].at[line(order, up(d), ("half", 1))], shift(d, 3)),
        ]

    def phase3a(u):
        order = ORDERS[UNITS[u][0]]
        arrived(u, 3)
        mine = hb[u].at[plane(order, pos[order[2]])]
        arriving[u, 4] = [send(u, k, mine, shift(order[2], by)) for k, by in ((7, 1), (8, 3))]

    def phase3b(u):
        order = ORDERS[UNITS[u][0]]
        arrived(u, 4)
        d = order[2]
        arriving[u, 5] = [
            send(u, 9, hb[u].at[plane(order, down(d), ("half", 0))], shift(d, 1)),
            send(u, 10, hb[u].at[plane(order, up(d), ("half", 1))], shift(d, 3)),
        ]

    begun = set()

    def multiply(u):
        o, kind, start, size = UNITS[u]
        arrived(u, 5)
        local[u].wait()
        lent[u].wait_recv()
        acc = acc_t if kind == "t" else acc_d
        first = kind not in begun
        begun.add(kind)

        def body(i, carry):
            side, col = lax.div(i, 2), pl.multiple_of(lax.rem(i, 2) * 256, 256)
            lhs = jnp.concatenate([hb[u][0].reshape(512, size), hb[u][1].reshape(512, size)], axis=1)
            rhs = wb[u][side, :, :, pl.ds(col, 256)].reshape(2 * size, 256)
            res = jnp.dot(lhs, rhs, preferred_element_type=jnp.float32)
            if first:
                acc[side, :, pl.ds(col, 256)] = res
            else:
                acc[side, :, pl.ds(col, 256)] += res
            return carry

        lax.fori_loop(0, 4, body, 0)

    def every(f, g):
        for u in range(3 * g, 3 * g + 3):
            f(u)

    def give(k, acc, part):
        copy = remote(acc.at[1], part, ps.at[k], pr.at[k], partner)
        copy.start()
        sends.append(copy)
        return copy

    def columns(row):
        return jnp.broadcast_to(row, (128, 128)).T

    def totals(acc, part, base):
        def body(j, carry):
            rows = pl.ds(pl.multiple_of(j * 128, 128), 128)
            logits = acc[0, rows, :] + part[rows, :]
            acc[0, rows, :] = logits
            tiles = [logits[:, 128 * t : 128 * t + 128] for t in range(4)]
            most = jnp.maximum(jnp.maximum(tiles[0], tiles[1]), jnp.maximum(tiles[2], tiles[3]))
            top = jnp.max(most.T, axis=0, keepdims=True)
            top_col = columns(top)
            e = [jnp.exp(t - top_col) for t in tiles]
            total = jnp.sum(((e[0] + e[1]) + (e[2] + e[3])).T, axis=0, keepdims=True)
            near[0, 8, pl.ds(base + j, 1), :] = top + jnp.log(total)
            return carry

        lax.fori_loop(0, 4, body, 0)

    near_me = pos["x"] * 2 + c
    far_me = pos["y"] * 4 + pos["z"]

    def spread(buf, ss, rs, r, me, count, value, targets):
        buf[r, me] = value
        copies = [remote(buf.at[r, me], buf.at[r, me], ss.at[r, i], rs.at[r], to) for i, to in enumerate(targets)]
        for copy in copies:
            copy.start()
        sends.extend(copies)
        full = buf.at[r, pl.ds(0, count - 1)]
        remote(full, full, ss.at[r, 0], rs.at[r], targets[0]).wait_recv()
        return buf[r, 0:count]

    near_to = [device(dx=a, dc=b) for a, b in near_offs]
    far_to = [device(dy=a, dz=b) for a, b in far_offs]

    def merge(values):
        top = jnp.max(values, axis=0)
        return top + jnp.log(jnp.sum(jnp.exp(values - top[None]), axis=0))

    for g in range(GROUPS):
        every(phase1, g)
    every(phase2a, 0)
    every(phase2a, 1)
    every(phase2b, 0)
    every(phase2a, 2)
    every(phase2a, 3)
    every(phase3a, 0)
    every(phase2b, 1)
    every(phase3a, 1)
    every(phase2b, 2)
    every(phase2b, 3)
    every(phase3b, 0)
    every(phase3a, 2)
    every(phase3b, 1)
    every(phase3a, 3)
    every(multiply, 0)
    gave_d = give(0, acc_d, part_d)
    every(phase3b, 2)
    every(multiply, 1)
    every(phase3b, 3)
    gave_d.wait_recv()
    totals(acc_d, part_d, 4)
    every(multiply, 2)
    every(multiply, 3)
    gave_t = give(1, acc_t, part_t)
    gave_t.wait_recv()
    totals(acc_t, part_t, 0)

    lse = merge(spread(near, ns, nr, 0, near_me, 8, near[0, 8], near_to))
    lse = merge(spread(far, fs, fr, 0, far_me, 16, lse, far_to))
    near[0, 8] = lse
    stat_ref[0:8, :] = lse

    out_t = pltpu.make_async_copy(acc_t.at[0], lt_ref, osem.at[0])
    out_d = pltpu.make_async_copy(acc_d.at[0], ld_ref, osem.at[1])
    out_t.start()
    out_d.start()

    offset = (w * 4 + n) * 512
    tok_f[...] = (tok_ref[...] - offset).astype(jnp.float32)

    def mass(j, carry):
        rows = pl.ds(pl.multiple_of(j * 128, 128), 128)
        lt, ld = acc_t[0, rows, :], acc_d[0, rows, :]
        t_col = columns(near[0, 8, pl.ds(j, 1), :])
        d_col = columns(near[0, 8, pl.ds(4 + j, 1), :])
        tok = columns(tok_f[pl.ds(j, 1), :])
        lanes = lax.broadcasted_iota(jnp.int32, (128, 128), 1).astype(jnp.float32)
        kept, picked = None, None
        for t in range(4):
            lp = lt[:, 128 * t : 128 * t + 128] - t_col
            dp = ld[:, 128 * t : 128 * t + 128] - d_col
            e = jnp.maximum(jnp.exp(lp) - jnp.exp(dp), 0.0)
            p = jnp.where(tok == lanes + 128.0 * t, lp - dp, 0.0)
            kept = e if kept is None else kept + e
            picked = p if picked is None else picked + p
        near[1, 8, pl.ds(j, 1), :] = jnp.sum(kept.T, axis=0, keepdims=True)
        near[1, 8, pl.ds(4 + j, 1), :] = jnp.sum(picked.T, axis=0, keepdims=True)
        return carry

    lax.fori_loop(0, 4, mass, 0)
    both = jnp.sum(spread(near, ns, nr, 1, near_me, 8, near[1, 8], near_to), axis=0)
    both = jnp.sum(spread(far, fs, fr, 1, far_me, 16, both, far_to), axis=0)
    stat_ref[8:12, :] = both[0:4]
    stat_ref[12:16, :] = jnp.exp(jnp.minimum(both[4:8], 0.0))

    out_t.wait()
    out_d.wait()
    for s in swaps + lent + sends:
        s.wait_send()


def on_device(target_hidden, target_weight, draft_hidden, draft_weight, draft_tokens):
    vmem, anywhere = pl.BlockSpec(memory_space=pltpu.VMEM), pl.BlockSpec(memory_space=pl.ANY)
    n_units = len(UNITS)
    dma = pltpu.SemaphoreType.DMA
    f32 = jnp.float32
    lt, ld, stat = pl.pallas_call(
        kernel,
        name="verify",
        out_shape=(
            jax.ShapeDtypeStruct((512, 512), f32),
            jax.ShapeDtypeStruct((512, 512), f32),
            jax.ShapeDtypeStruct((16, 128), f32),
        ),
        in_specs=[anywhere, anywhere, anywhere, anywhere, vmem],
        out_specs=(anywhere, anywhere, vmem),
        scratch_shapes=(
            [pltpu.VMEM((2, 4, 4, 2, 16, size), jnp.bfloat16) for _, _, _, size in UNITS]
            + [pltpu.VMEM((2, 2, size, 512), jnp.bfloat16) for _, _, _, size in UNITS]
            + [
                pltpu.VMEM((4, 4, 4096), jnp.bfloat16),
                pltpu.VMEM((4, 4, 1024), jnp.bfloat16),
                pltpu.VMEM((2, 512, 512), f32),
                pltpu.VMEM((2, 512, 512), f32),
                pltpu.VMEM((512, 512), f32),
                pltpu.VMEM((512, 512), f32),
                pltpu.VMEM((4, 128), f32),
                pltpu.VMEM((2, 9, 8, 128), f32),
                pltpu.VMEM((2, 16, 8, 128), f32),
                dma((n_units, 11)), dma((n_units, 11)),
                dma((n_units,)), dma((n_units,)), dma((n_units,)),
                dma((2, 4)), dma((2, 4)), dma((2,)),
                dma((2,)), dma((2,)),
                dma((2, 7)), dma((2,)),
                dma((2, 15)), dma((2,)),
                dma((2,)),
            ]
        ),
        compiler_params=pltpu.CompilerParams(
            collective_id=0, has_side_effects=True, vmem_limit_bytes=56 * 2**20
        ),
    )(
        target_hidden,
        target_weight.reshape(2, 2, 4096, 512),
        draft_hidden,
        draft_weight.reshape(2, 2, 1024, 512),
        draft_tokens.reshape(4, 128),
    )
    t_norm = stat[0:4].reshape(512, 1)
    d_norm = stat[4:8].reshape(512, 1)
    leftover = stat[8:12].reshape(512)
    t_log, d_log = lt - t_norm, ld - d_norm
    excess = jnp.maximum(jnp.exp(t_log) - jnp.exp(d_log), 0.0)
    residual = excess / jnp.maximum(leftover, 0.25)[:, None]
    return t_log, d_log, residual, stat[12:16].reshape(512), leftover


def solution(mesh):
    placed = (
        P(("wide", "narrow"), None),
        P(None, ("wide", "narrow")),
        P(("wide", "narrow"), None),
        P(None, ("wide", "narrow")),
        P(),
    )
    return jax.shard_map(
        on_device,
        mesh=mesh,
        in_specs=placed,
        out_specs=(
            P(None, ("wide", "narrow")),
            P(None, ("wide", "narrow")),
            P(None, ("wide", "narrow")),
            P(),
            P(),
        ),
        check_vma=False,
    )
```

```python
import functools

import jax
import jax.numpy as jnp
from jax import lax
from jax.experimental import pallas as pl
from jax.experimental.pallas import tpu as pltpu
from jax.sharding import PartitionSpec as P

MESH = pl.DeviceIdType.MESH
T = 128
ORDERS = (("x", "y", "z"), ("y", "z", "x"), ("z", "x", "y"))
SPLIT = (("d", (3, 3, 2)), ("t", (4, 4, 4)), ("t", (3, 3, 4)), ("t", (2, 2, 2)), ("t", (1, 1, 2)))


def make_units():
    units, used = [], {"d": 0, "t": 0}
    for kind, sizes in SPLIT:
        for order, size in enumerate(sizes):
            units.append((order, kind, used[kind] * T, size * T))
            used[kind] += size
    return units


UNITS = make_units()
GROUPS = len(SPLIT)


def view(sel):
    whole = slice(None)
    x = sel["x"]
    if x == "all":
        hi, lo = whole, whole
    elif isinstance(x, tuple):
        hi, lo = whole, x[1]
    else:
        hi, lo = lax.div(x, 2), lax.rem(x, 2)
    rest = []
    for name in ("y", "z"):
        v = sel[name]
        if isinstance(v, str):
            rest.append(whole)
        elif isinstance(v, tuple):
            rest.append(pl.ds(2 * v[1], 2))
        else:
            rest.append(v)
    return (lo, rest[0], rest[1], hi)


def kernel(ht_ref, wt_ref, hd_ref, wd_ref, tok_ref, lt_ref, ld_ref, ex_ref, stat_ref, *scratch):
    n_units = len(UNITS)
    hb = scratch[:n_units]
    wb = scratch[n_units : 2 * n_units]
    (stage_t, stage_d, acc_t, acc_d, part_t, part_d, tok_i, tok_f, near, far,
     gs, gr, wl, ws, wr, es, er, el, ps, pr, ns, nr, fs, fr) = scratch[2 * n_units :]
    w, n = lax.axis_index("wide"), lax.axis_index("narrow")
    pos = {"x": lax.div(n, 2) * 2 + lax.rem(w, 2), "y": lax.div(w, 8), "z": lax.rem(lax.div(w, 2), 4)}
    c = lax.rem(n, 2)

    def device(dx=0, dy=0, dz=0, dc=0):
        x = lax.rem(pos["x"] + dx, 4)
        y = lax.rem(pos["y"] + dy, 4)
        z = lax.rem(pos["z"] + dz, 4)
        return ((y * 4 + z) * 2 + lax.rem(x, 2), lax.div(x, 2) * 2 + lax.rem(c + dc, 2))

    def shift(dim, by):
        return device(**{"d" + dim: by})

    def remote(src, dst, send, recv, to):
        return pltpu.make_async_remote_copy(
            src_ref=src, dst_ref=dst, send_sem=send, recv_sem=recv, device_id=to, device_id_type=MESH
        )

    partner = device(dc=1)
    xh, xl = lax.div(pos["x"], 2), lax.rem(pos["x"], 2)
    me = xl * 2 + c

    local = []
    for u, (order, kind, start, size) in enumerate(UNITS):
        ref = wt_ref if kind == "t" else wd_ref
        local.append(pltpu.make_async_copy(ref.at[c, :, pl.ds(start, size), :], wb[u].at[0], wl.at[u]))
        local[-1].start()
    own_t = pltpu.make_async_copy(
        ht_ref.at[:, pl.ds(pl.multiple_of(c * 8192 + xl * 4096, T), 4096)], stage_t.at[me], el.at[0])
    own_d = pltpu.make_async_copy(
        hd_ref.at[:, pl.ds(pl.multiple_of(c * 2048 + xl * 1024, T), 1024)], stage_d.at[me], el.at[1])
    own_tok = pltpu.make_async_copy(tok_ref, tok_i, el.at[2])
    own_t.start()
    own_d.start()
    own_tok.start()

    steps = (0, 1, 2, 1)
    near_offs = sorted(((a, b) for a in range(4) for b in range(2) if (a, b) != (0, 0)), key=lambda o: -2 * steps[o[0]] - o[1])
    far_offs = sorted(((a, b) for a in range(4) for b in range(4) if (a, b) != (0, 0)), key=lambda o: -steps[o[0]] - steps[o[1]])
    barrier = pltpu.get_barrier_semaphore()
    for a, b in near_offs:
        pl.semaphore_signal(barrier, inc=1, device_id=device(dx=a, dc=b), device_id_type=MESH)
    for a, b in far_offs:
        pl.semaphore_signal(barrier, inc=1, device_id=device(dy=a, dz=b), device_id_type=MESH)
    pl.semaphore_wait(barrier, len(near_offs) + len(far_offs))

    swaps = []
    for j in range(1, 4):
        to = lax.rem(me + j, 4)
        to_c, to_l = lax.rem(to, 2), lax.div(to, 2)
        target = ((pos["y"] * 4 + pos["z"]) * 2 + to_l, xh * 2 + to_c)
        qt = pl.multiple_of(to_c * 8192 + to_l * 4096, T)
        qd = pl.multiple_of(to_c * 2048 + to_l * 1024, T)
        swaps.append(remote(hd_ref.at[:, pl.ds(qd, 1024)], stage_d.at[me], es.at[1, j], er.at[1, j], target))
        swaps.append(remote(ht_ref.at[:, pl.ds(qt, 4096)], stage_t.at[me], es.at[0, j], er.at[0, j], target))
    for s in swaps:
        s.start()
    lent = []
    for u, (order, kind, start, size) in enumerate(UNITS):
        ref = wt_ref if kind == "t" else wd_ref
        lent.append(remote(ref.at[1 - c, :, pl.ds(start, size), :], wb[u].at[1], ws.at[u], wr.at[u], partner))
        lent[-1].start()
    own_t.wait()
    own_d.wait()
    for s in swaps:
        s.wait_recv()

    sends = []

    def send(u, k, src, to):
        copy = remote(src, src, gs.at[u, k], gr.at[u, k], to)
        copy.start()
        sends.append(copy)
        return copy

    arriving = {}

    def line(order, c2, part="all"):
        d1, d2, d3 = order
        return view({d1: part, d2: c2, d3: pos[d3]})

    def plane(order, c3, part="all"):
        d1, d2, d3 = order
        return view({d1: "all", d2: part, d3: c3})

    def up(dim):
        return lax.rem(pos[dim] + 1, 4)

    def down(dim):
        return lax.rem(pos[dim] + 3, 4)

    def phase1(u):
        o, kind, start, size = UNITS[u]
        order = ORDERS[o]
        stage = stage_t if kind == "t" else stage_d
        rows = [stage[j, :, start : start + size].astype(jnp.float32) for j in range(4)]
        hb[u][xl, pos["y"], pos["z"], xh] = jnp.concatenate(rows, axis=0).astype(jnp.bfloat16)
        mine = hb[u].at[xl, pos["y"], pos["z"], xh]
        arriving[u, 1] = [send(u, k, mine, shift(order[0], by)) for k, by in ((0, 1), (1, 3), (2, 2))]

    def arrived(u, phase):
        for copy in arriving[u, phase]:
            copy.wait_recv()

    def phase2a(u):
        order = ORDERS[UNITS[u][0]]
        arrived(u, 1)
        mine = hb[u].at[line(order, pos[order[1]])]
        arriving[u, 2] = [send(u, k, mine, shift(order[1], by)) for k, by in ((3, 1), (4, 3))]

    def phase2b(u):
        order = ORDERS[UNITS[u][0]]
        arrived(u, 2)
        d = order[1]
        arriving[u, 3] = [
            send(u, 5, hb[u].at[line(order, down(d), ("half", 0))], shift(d, 1)),
            send(u, 6, hb[u].at[line(order, up(d), ("half", 1))], shift(d, 3)),
        ]

    def phase3a(u):
        order = ORDERS[UNITS[u][0]]
        arrived(u, 3)
        mine = hb[u].at[plane(order, pos[order[2]])]
        arriving[u, 4] = [send(u, k, mine, shift(order[2], by)) for k, by in ((7, 1), (8, 3))]

    def phase3b(u):
        order = ORDERS[UNITS[u][0]]
        arrived(u, 4)
        d = order[2]
        arriving[u, 5] = [
            send(u, 9, hb[u].at[plane(order, down(d), ("half", 0))], shift(d, 1)),
            send(u, 10, hb[u].at[plane(order, up(d), ("half", 1))], shift(d, 3)),
        ]

    begun = set()

    def multiply(u, sides=(1, 0), again=False):
        o, kind, start, size = UNITS[u]
        if not again:
            arrived(u, 5)
            local[u].wait()
            lent[u].wait_recv()
        acc = acc_t if kind == "t" else acc_d
        first = kind not in begun
        begun.add(kind)
        lhs = jnp.concatenate([hb[u][0].reshape(512, size), hb[u][1].reshape(512, size)], axis=1)
        for side in sides:
            for col in (0, 256):
                rhs = wb[u][side, :, :, col : col + 256].reshape(2 * size, 256)
                res = jnp.dot(lhs, rhs, preferred_element_type=jnp.float32)
                if first:
                    acc[side, :, col : col + 256] = res
                else:
                    acc[side, :, col : col + 256] += res

    def every(f, g):
        for u in range(3 * g, 3 * g + 3):
            f(u)

    def given(k, acc, part, j):
        rows = pl.ds(pl.multiple_of(j * 128, 128), 128)
        return remote(acc.at[1, rows, :], part.at[rows, :], ps.at[k, j], pr.at[k, j], partner)

    def give(k, acc, part):
        for j in range(4):
            sends.append(given(k, acc, part, j))
            sends[-1].start()

    def columns(row):
        return jnp.broadcast_to(row, (128, 128)).T

    def totals(k, acc, part, base):
        def body(j, carry):
            rows = pl.ds(pl.multiple_of(j * 128, 128), 128)
            given(k, acc, part, j).wait_recv()
            mixed = acc[0, rows, :] + part[rows, :]
            order = [32 * q + r for q in range(4) for r in (0, 16, 8, 24)]
            logits = jnp.concatenate([mixed[r : r + 8] for r in order], axis=0)
            acc[0, rows, :] = logits
            tiles = [logits[:, 128 * t : 128 * t + 128] for t in range(4)]
            most = jnp.maximum(jnp.maximum(tiles[0], tiles[1]), jnp.maximum(tiles[2], tiles[3]))
            top = jnp.max(most.T, axis=0, keepdims=True)
            top_col = columns(top)
            e = [jnp.exp(t - top_col) for t in tiles]
            total = jnp.sum(((e[0] + e[1]) + (e[2] + e[3])).T, axis=0, keepdims=True)
            near[0, 8, pl.ds(base + j, 1), :] = top + jnp.log(total)
            return carry

        lax.fori_loop(0, 4, body, 0)

    near_me = pos["x"] * 2 + c
    far_me = pos["y"] * 4 + pos["z"]

    def spread(buf, ss, rs, r, me, count, value, targets):
        buf[r, me] = value
        copies = [remote(buf.at[r, me], buf.at[r, me], ss.at[r, i], rs.at[r], to) for i, to in enumerate(targets)]
        for copy in copies:
            copy.start()
        sends.extend(copies)
        full = buf.at[r, pl.ds(0, count - 1)]
        remote(full, full, ss.at[r, 0], rs.at[r], targets[0]).wait_recv()
        return buf[r, 0:count]

    near_to = [device(dx=a, dc=b) for a, b in near_offs]
    far_to = [device(dy=a, dz=b) for a, b in far_offs]

    def merge(values):
        top = jnp.max(values, axis=0)
        return top + jnp.log(jnp.sum(jnp.exp(values - top[None]), axis=0))

    for phase in (phase1, phase2a, phase2b):
        for g in range(GROUPS):
            every(phase, g)
    every(phase3a, 0)
    every(phase3a, 1)
    every(phase3b, 0)
    every(phase3a, 2)
    every(phase3b, 1)
    every(phase3a, 3)
    every(multiply, 0)
    give(0, acc_d, part_d)
    every(phase3b, 2)
    every(phase3a, 4)
    every(multiply, 1)
    every(phase3b, 3)
    totals(0, acc_d, part_d, 4)
    every(phase3b, 4)
    every(multiply, 2)
    every(multiply, 3)
    every(lambda u: multiply(u, (1,)), 4)
    give(1, acc_t, part_t)
    every(lambda u: multiply(u, (0,), True), 4)
    totals(1, acc_t, part_t, 0)

    lse = merge(spread(near, ns, nr, 0, near_me, 8, near[0, 8], near_to))
    lse = merge(spread(far, fs, fr, 0, far_me, 16, lse, far_to))
    near[0, 8] = lse

    own_tok.wait()
    offset = (w * 4 + n) * 512
    tok_f[...] = (tok_i[...] - offset).astype(jnp.float32)

    def mass(j, carry):
        rows = pl.ds(pl.multiple_of(j * 128, 128), 128)
        lt, ld = acc_t[0, rows, :], acc_d[0, rows, :]
        t_col = columns(near[0, 8, pl.ds(j, 1), :])
        d_col = columns(near[0, 8, pl.ds(4 + j, 1), :])
        tok = columns(tok_f[pl.ds(j, 1), :])
        lanes = lax.broadcasted_iota(jnp.int32, (128, 128), 1).astype(jnp.float32)
        kept, picked = None, None
        for t in range(4):
            lp = lt[:, 128 * t : 128 * t + 128] - t_col
            dp = ld[:, 128 * t : 128 * t + 128] - d_col
            lt_ref[rows, 128 * t : 128 * t + 128] = lp
            ld_ref[rows, 128 * t : 128 * t + 128] = dp
            e = jnp.maximum(jnp.exp(lp) - jnp.exp(dp), 0.0)
            ex_ref[rows, 128 * t : 128 * t + 128] = e
            p = jnp.where(tok == lanes + 128.0 * t, lp - dp, 0.0)
            kept = e if kept is None else kept + e
            picked = p if picked is None else picked + p
        near[1, 8, pl.ds(j, 1), :] = jnp.sum(kept.T, axis=0, keepdims=True)
        near[1, 8, pl.ds(4 + j, 1), :] = jnp.sum(picked.T, axis=0, keepdims=True)
        return carry

    lax.fori_loop(0, 4, mass, 0)
    both = jnp.sum(spread(near, ns, nr, 1, near_me, 8, near[1, 8], near_to), axis=0)
    both = jnp.sum(spread(far, fs, fr, 1, far_me, 16, both, far_to), axis=0)
    stat_ref[...] = both

    for s in swaps + lent + sends:
        s.wait_send()


def finish(lt_ref, ld_ref, ex_ref, stat_ref, t_ref, d_ref, r_ref, accept_ref, left_ref, res, sem):
    copies = [pltpu.make_async_copy(lt_ref, t_ref, sem.at[0]), pltpu.make_async_copy(ld_ref, d_ref, sem.at[1])]
    for copy in copies:
        copy.start()
    left = stat_ref[0:4, :]
    left_ref[...] = left
    accept_ref[...] = jnp.exp(jnp.minimum(stat_ref[4:8, :], 0.0))
    scale = 1.0 / jnp.maximum(left, 0.25)
    for j in range(4):
        rows = slice(128 * j, 128 * j + 128)
        col = jnp.broadcast_to(scale[j : j + 1], (128, 128)).T
        for t in range(4):
            cols = slice(128 * t, 128 * t + 128)
            res[rows, cols] = ex_ref[rows, cols] * col
        copies.append(pltpu.make_async_copy(res.at[rows], r_ref.at[rows], sem.at[2 + j]))
        copies[-1].start()
    for copy in copies:
        copy.wait()


def on_device(target_hidden, target_weight, draft_hidden, draft_weight, draft_tokens):
    vmem, anywhere = pl.BlockSpec(memory_space=pltpu.VMEM), pl.BlockSpec(memory_space=pl.ANY)
    n_units = len(UNITS)
    dma = pltpu.SemaphoreType.DMA
    f32 = jnp.float32
    lt, ld, ex, stat = pl.pallas_call(
        kernel,
        name="verify",
        out_shape=(
            pltpu.VMEM((512, 512), f32),
            pltpu.VMEM((512, 512), f32),
            pltpu.VMEM((512, 512), f32),
            pltpu.VMEM((8, 128), f32),
        ),
        in_specs=[anywhere] * 5,
        out_specs=(vmem, vmem, vmem, vmem),
        scratch_shapes=(
            [pltpu.VMEM((2, 4, 4, 2, 16, size), jnp.bfloat16) for _, _, _, size in UNITS]
            + [pltpu.VMEM((2, 2, size, 512), jnp.bfloat16) for _, _, _, size in UNITS]
            + [
                pltpu.VMEM((4, 4, 4096), jnp.bfloat16),
                pltpu.VMEM((4, 4, 1024), jnp.bfloat16),
                pltpu.VMEM((2, 512, 512), f32),
                pltpu.VMEM((2, 512, 512), f32),
                pltpu.VMEM((512, 512), f32),
                pltpu.VMEM((512, 512), f32),
                pltpu.VMEM((4, 128), jnp.int32),
                pltpu.VMEM((4, 128), f32),
                pltpu.VMEM((2, 9, 8, 128), f32),
                pltpu.VMEM((2, 16, 8, 128), f32),
                dma((n_units, 11)), dma((n_units, 11)),
                dma((n_units,)), dma((n_units,)), dma((n_units,)),
                dma((2, 4)), dma((2, 4)), dma((3,)),
                dma((2, 4)), dma((2, 4)),
                dma((2, 7)), dma((2,)),
                dma((2, 15)), dma((2,)),
            ]
        ),
        compiler_params=pltpu.CompilerParams(
            collective_id=0, has_side_effects=True, vmem_limit_bytes=48 * 2**20
        ),
    )(*[
        pltpu.with_memory_space_constraint(a, pltpu.HBM)
        for a in (
            target_hidden,
            target_weight.reshape(2, 2, 4096, 512),
            draft_hidden,
            draft_weight.reshape(2, 2, 1024, 512),
            draft_tokens.reshape(4, 128),
        )
    ])
    whole = jax.ShapeDtypeStruct((512, 512), f32)
    small = jax.ShapeDtypeStruct((4, 128), f32)
    held = [pltpu.with_memory_space_constraint(a, pltpu.VMEM) for a in (lt, ld, ex, stat)]
    t_log, d_log, residual, acceptance, leftover = pl.pallas_call(
        finish,
        name="finish",
        out_shape=(whole, whole, whole, small, small),
        in_specs=[vmem] * 4,
        out_specs=(anywhere, anywhere, anywhere, vmem, vmem),
        scratch_shapes=[pltpu.VMEM((512, 512), f32), dma((6,))],
        compiler_params=pltpu.CompilerParams(vmem_limit_bytes=8 * 2**20),
    )(*held)
    return t_log, d_log, residual, acceptance.reshape(512), leftover.reshape(512)


def solution(mesh):
    placed = (
        P(("wide", "narrow"), None),
        P(None, ("wide", "narrow")),
        P(("wide", "narrow"), None),
        P(None, ("wide", "narrow")),
        P(),
    )
    return jax.shard_map(
        on_device,
        mesh=mesh,
        in_specs=placed,
        out_specs=(
            P(None, ("wide", "narrow")),
            P(None, ("wide", "narrow")),
            P(None, ("wide", "narrow")),
            P(),
            P(),
        ),
        check_vma=False,
    )
```

```python
import functools

import jax
import jax.numpy as jnp
from jax import lax
from jax.experimental import pallas as pl
from jax.experimental.pallas import tpu as pltpu
from jax.sharding import PartitionSpec as P

MESH = pl.DeviceIdType.MESH
T = 128
ORDERS = (("x", "y", "z"), ("y", "z", "x"), ("z", "x", "y"))
SPLIT = (("d", (3, 3, 2)), ("t", (4, 4, 4)), ("t", (3, 3, 4)), ("t", (2, 2, 2)), ("t", (1, 1, 2)))


def make_units():
    units, used = [], {"d": 0, "t": 0}
    for kind, sizes in SPLIT:
        for order, size in enumerate(sizes):
            units.append((order, kind, used[kind] * T, size * T))
            used[kind] += size
    return units


UNITS = make_units()
GROUPS = len(SPLIT)


def view(sel):
    whole = slice(None)
    x = sel["x"]
    if x == "all":
        hi, lo = whole, whole
    elif isinstance(x, tuple):
        hi, lo = whole, x[1]
    else:
        hi, lo = lax.div(x, 2), lax.rem(x, 2)
    rest = []
    for name in ("y", "z"):
        v = sel[name]
        if isinstance(v, str):
            rest.append(whole)
        elif isinstance(v, tuple):
            rest.append(pl.ds(2 * v[1], 2))
        else:
            rest.append(v)
    return (lo, rest[0], rest[1], hi)


def kernel(ht_ref, wt_ref, hd_ref, wd_ref, tok_ref, lt_ref, ld_ref, ex_ref, stat_ref, *scratch):
    n_units = len(UNITS)
    hb = scratch[:n_units]
    wb = scratch[n_units : 2 * n_units]
    (hid_t, hid_d, stage_t, stage_d, acc_t, acc_d, part_t, part_d, tok_i, tok_f, tops, near, far,
     gs, gr, ws, wr, es, er, el, ps, pr, ns, nr, fs, fr) = scratch[2 * n_units :]
    w, n = lax.axis_index("wide"), lax.axis_index("narrow")
    pos = {"x": lax.div(n, 2) * 2 + lax.rem(w, 2), "y": lax.div(w, 8), "z": lax.rem(lax.div(w, 2), 4)}
    c = lax.rem(n, 2)

    def device(dx=0, dy=0, dz=0, dc=0):
        x = lax.rem(pos["x"] + dx, 4)
        y = lax.rem(pos["y"] + dy, 4)
        z = lax.rem(pos["z"] + dz, 4)
        return ((y * 4 + z) * 2 + lax.rem(x, 2), lax.div(x, 2) * 2 + lax.rem(c + dc, 2))

    def shift(dim, by):
        return device(**{"d" + dim: by})

    def remote(src, dst, send, recv, to):
        return pltpu.make_async_remote_copy(
            src_ref=src, dst_ref=dst, send_sem=send, recv_sem=recv, device_id=to, device_id_type=MESH
        )

    partner = device(dc=1)
    xh, xl = lax.div(pos["x"], 2), lax.rem(pos["x"], 2)
    me = xl * 2 + c

    got_t = pltpu.make_async_copy(ht_ref, hid_t, el.at[0])
    got_d = pltpu.make_async_copy(hd_ref, hid_d, el.at[1])
    got_tok = pltpu.make_async_copy(tok_ref, tok_i, el.at[2])
    got_d.start()
    got_t.start()
    got_tok.start()

    steps = (0, 1, 2, 1)
    near_offs = sorted(((a, b) for a in range(4) for b in range(2) if (a, b) != (0, 0)), key=lambda o: -2 * steps[o[0]] - o[1])
    far_offs = sorted(((a, b) for a in range(4) for b in range(4) if (a, b) != (0, 0)), key=lambda o: -steps[o[0]] - steps[o[1]])
    barrier = pltpu.get_barrier_semaphore()
    for a, b in near_offs:
        pl.semaphore_signal(barrier, inc=1, device_id=device(dx=a, dc=b), device_id_type=MESH)
    for a, b in far_offs:
        pl.semaphore_signal(barrier, inc=1, device_id=device(dy=a, dz=b), device_id_type=MESH)
    for u, (order, kind, start, size) in enumerate(UNITS):
        ref = wt_ref if kind == "t" else wd_ref
        pltpu.make_async_copy(ref.at[c, :, pl.ds(start, size), :], wb[u].at[0], wr.at[u]).start()
    got_d.wait()
    got_t.wait()
    pl.semaphore_wait(barrier, len(near_offs) + len(far_offs))

    swaps = []
    for j in range(1, 4):
        to = lax.rem(me + j, 4)
        to_c, to_l = lax.rem(to, 2), lax.div(to, 2)
        target = ((pos["y"] * 4 + pos["z"]) * 2 + to_l, xh * 2 + to_c)
        qt = pl.multiple_of(to_c * 8192 + to_l * 4096, T)
        qd = pl.multiple_of(to_c * 2048 + to_l * 1024, T)
        swaps.append(remote(hid_d.at[:, pl.ds(qd, 1024)], stage_d.at[me], es.at[1, j], er.at[1, j], target))
        swaps.append(remote(hid_t.at[:, pl.ds(qt, 4096)], stage_t.at[me], es.at[0, j], er.at[0, j], target))
    for s in swaps:
        s.start()
    own_t = pltpu.make_async_copy(
        hid_t.at[:, pl.ds(pl.multiple_of(c * 8192 + xl * 4096, T), 4096)], stage_t.at[me], el.at[0])
    own_d = pltpu.make_async_copy(
        hid_d.at[:, pl.ds(pl.multiple_of(c * 2048 + xl * 1024, T), 1024)], stage_d.at[me], el.at[1])
    own_t.start()
    own_d.start()
    lent = []
    for u, (order, kind, start, size) in enumerate(UNITS):
        ref = wt_ref if kind == "t" else wd_ref
        lent.append(remote(ref.at[1 - c, :, pl.ds(start, size), :], wb[u].at[1], ws.at[u], wr.at[u], partner))
        lent[-1].start()
    own_t.wait()
    own_d.wait()
    for s in swaps:
        s.wait_recv()

    sends = []

    def send(u, phase, src, to):
        remote(src, src, gs.at[u], gr.at[u, phase], to).start()

    def arrived(u, phase):
        got = (
            hb[u].at[0, 0, pl.ds(0, 3), 0],
            hb[u].at[0, 0],
            hb[u].at[0, 0, pl.ds(0, 2)],
            hb[u].at[0],
            hb[u].at[0, pl.ds(0, 2)],
        )[phase]
        remote(got, got, gs.at[u], gr.at[u, phase], partner).wait_recv()

    def sent(u):
        all63 = part_t.at[pl.ds(0, 504), pl.ds(0, UNITS[u][3])]
        remote(all63, all63, gs.at[u], gr.at[u, 0], partner).wait_send()

    def line(order, c2, part="all"):
        d1, d2, d3 = order
        return view({d1: part, d2: c2, d3: pos[d3]})

    def plane(order, c3, part="all"):
        d1, d2, d3 = order
        return view({d1: "all", d2: part, d3: c3})

    def up(dim):
        return lax.rem(pos[dim] + 1, 4)

    def down(dim):
        return lax.rem(pos[dim] + 3, 4)

    def phase1(u):
        o, kind, start, size = UNITS[u]
        order = ORDERS[o]
        stage = stage_t if kind == "t" else stage_d
        rows = [stage[j, :, start : start + size].astype(jnp.float32) for j in range(4)]
        hb[u][xl, pos["y"], pos["z"], xh] = jnp.concatenate(rows, axis=0).astype(jnp.bfloat16)
        mine = hb[u].at[xl, pos["y"], pos["z"], xh]
        for by in (2, 1, 3):
            send(u, 0, mine, shift(order[0], by))

    def phase2a(u):
        order = ORDERS[UNITS[u][0]]
        arrived(u, 0)
        mine = hb[u].at[line(order, pos[order[1]])]
        for by in (1, 3):
            send(u, 1, mine, shift(order[1], by))

    def phase2b(u):
        order = ORDERS[UNITS[u][0]]
        arrived(u, 1)
        d = order[1]
        send(u, 2, hb[u].at[line(order, down(d), ("half", 0))], shift(d, 1))
        send(u, 2, hb[u].at[line(order, up(d), ("half", 1))], shift(d, 3))

    def phase3a(u):
        order = ORDERS[UNITS[u][0]]
        arrived(u, 2)
        mine = hb[u].at[plane(order, pos[order[2]])]
        for by in (1, 3):
            send(u, 3, mine, shift(order[2], by))

    def phase3b(u):
        order = ORDERS[UNITS[u][0]]
        arrived(u, 3)
        d = order[2]
        send(u, 4, hb[u].at[plane(order, down(d), ("half", 0))], shift(d, 1))
        send(u, 4, hb[u].at[plane(order, up(d), ("half", 1))], shift(d, 3))

    begun = set()

    def multiply(u, sides=(1, 0), again=False):
        o, kind, start, size = UNITS[u]
        if not again:
            arrived(u, 4)
            remote(wb[u], wb[u], ws.at[u], wr.at[u], partner).wait_recv()
        acc = acc_t if kind == "t" else acc_d
        first = kind not in begun
        begun.add(kind)
        lhs = jnp.concatenate([hb[u][0].reshape(512, size), hb[u][1].reshape(512, size)], axis=1)
        for side in sides:
            for col in (0, 256):
                rhs = wb[u][side, :, :, col : col + 256].reshape(2 * size, 256)
                res = jnp.dot(lhs, rhs, preferred_element_type=jnp.float32)
                if first:
                    acc[side, :, col : col + 256] = res
                else:
                    acc[side, :, col : col + 256] += res

    def every(f, g):
        for u in range(3 * g, 3 * g + 3):
            f(u)

    def given(k, acc, part, j):
        rows = pl.ds(pl.multiple_of(j * 128, 128), 128)
        return remote(acc.at[1, rows, :], part.at[rows, :], ps.at[k, j], pr.at[k, j], partner)

    def give(k, acc, part):
        for j in range(4):
            sends.append(given(k, acc, part, j))
            sends[-1].start()

    def columns(row):
        return jnp.broadcast_to(row, (128, 128)).T

    def totals(k, acc, part, base):
        def body(j, carry):
            rows = pl.ds(pl.multiple_of(j * 128, 128), 128)
            given(k, acc, part, j).wait_recv()
            mixed = acc[0, rows, :] + part[rows, :]
            order = [32 * q + r for q in range(4) for r in (0, 16, 8, 24)]
            logits = jnp.concatenate([mixed[r : r + 8] for r in order], axis=0)
            acc[0, rows, :] = logits
            tiles = [logits[:, 128 * t : 128 * t + 128] for t in range(4)]
            most = jnp.maximum(jnp.maximum(tiles[0], tiles[1]), jnp.maximum(tiles[2], tiles[3]))
            top = jnp.max(most.T, axis=0, keepdims=True)
            top_col = columns(top)
            e = [jnp.exp(t - top_col) for t in tiles]
            part[rows, :] = jnp.concatenate(e, axis=1)
            tops[pl.ds(base + j, 1), :] = top
            total = jnp.sum(((e[0] + e[1]) + (e[2] + e[3])).T, axis=0, keepdims=True)
            near[0, 8, pl.ds(base + j, 1), :] = top + jnp.log(total)
            return carry

        lax.fori_loop(0, 4, body, 0)

    near_me = pos["x"] * 2 + c
    far_me = pos["y"] * 4 + pos["z"]

    def spread(buf, ss, rs, r, me, count, value, targets):
        buf[r, me] = value
        for to in targets:
            remote(buf.at[r, me], buf.at[r, me], ss.at[r], rs.at[r], to).start()

    def others(buf, ss, rs, r, count, targets):
        full = buf.at[r, pl.ds(0, count - 1)]
        return remote(full, full, ss.at[r], rs.at[r], targets[0])

    def gathered(buf, ss, rs, r, count, targets):
        others(buf, ss, rs, r, count, targets).wait_recv()
        return buf[r, 0:count]

    near_to = [device(dx=a, dc=b) for a, b in near_offs]
    far_to = [device(dy=a, dz=b) for a, b in far_offs]
    near_all = lambda r: (near, ns, nr, r, 8, near_to)
    far_all = lambda r: (far, fs, fr, r, 16, far_to)

    def merge(values):
        top = jnp.max(values, axis=0)
        return top + jnp.log(jnp.sum(jnp.exp(values - top[None]), axis=0))

    for phase in (phase1, phase2a, phase2b):
        for g in range(GROUPS):
            every(phase, g)
    every(phase3a, 0)
    every(phase3a, 1)
    every(phase3b, 0)
    every(phase3a, 2)
    every(phase3b, 1)
    every(phase3a, 3)
    every(multiply, 0)
    give(0, acc_d, part_d)
    every(phase3b, 2)
    every(phase3a, 4)
    every(multiply, 1)
    every(phase3b, 3)
    totals(0, acc_d, part_d, 4)
    every(phase3b, 4)
    every(multiply, 2)
    every(multiply, 3)
    every(lambda u: multiply(u, (1,)), 4)
    give(1, acc_t, part_t)
    every(lambda u: multiply(u, (0,), True), 4)
    totals(1, acc_t, part_t, 0)

    spread(near, ns, nr, 0, near_me, 8, near[0, 8], near_to)
    got_tok.wait()
    tok_f[...] = (tok_i[...] - (w * 4 + n) * 512).astype(jnp.float32)

    def pick(j, carry):
        rows = pl.ds(pl.multiple_of(j * 128, 128), 128)
        tok = columns(tok_f[pl.ds(j, 1), :])
        lanes = lax.broadcasted_iota(jnp.int32, (128, 128), 1).astype(jnp.float32)
        picked = None
        for t in range(4):
            cols = slice(128 * t, 128 * t + 128)
            p = jnp.where(tok == lanes + 128.0 * t, acc_t[0, rows, cols] - acc_d[0, rows, cols], 0.0)
            picked = p if picked is None else picked + p
        near[1, 8, pl.ds(4 + j, 1), :] = jnp.sum(picked.T, axis=0, keepdims=True)
        return carry

    lax.fori_loop(0, 4, pick, 0)
    lse = merge(gathered(*near_all(0)))
    spread(far, fs, fr, 0, far_me, 16, lse, far_to)
    lse = merge(gathered(*far_all(0)))
    near[0, 8] = lse
    tops[...] = jnp.exp(tops[...] - lse)

    def mass(j, carry):
        rows = pl.ds(pl.multiple_of(j * 128, 128), 128)
        t_col = columns(tops[pl.ds(j, 1), :])
        d_col = columns(tops[pl.ds(4 + j, 1), :])
        kept = None
        for t in range(4):
            cols = slice(128 * t, 128 * t + 128)
            e = jnp.maximum(part_t[rows, cols] * t_col - part_d[rows, cols] * d_col, 0.0)
            ex_ref[rows, cols] = e
            kept = e if kept is None else kept + e
        near[1, 8, pl.ds(j, 1), :] = jnp.sum(kept.T, axis=0, keepdims=True)
        return carry

    lax.fori_loop(0, 4, mass, 0)

    spread(near, ns, nr, 1, near_me, 8, near[1, 8], near_to)

    def normalize(j, carry):
        rows = pl.ds(pl.multiple_of(j * 128, 128), 128)
        t_col = columns(near[0, 8, pl.ds(j, 1), :])
        d_col = columns(near[0, 8, pl.ds(4 + j, 1), :])
        for t in range(4):
            cols = slice(128 * t, 128 * t + 128)
            lt_ref[rows, cols] = acc_t[0, rows, cols] - t_col
            ld_ref[rows, cols] = acc_d[0, rows, cols] - d_col
        return carry

    lax.fori_loop(0, 4, normalize, 0)
    both = jnp.sum(gathered(*near_all(1)), axis=0)
    spread(far, fs, fr, 1, far_me, 16, both, far_to)
    both = jnp.sum(gathered(*far_all(1)), axis=0)
    stat_ref[0:4, :] = both[0:4]
    stat_ref[4:8, :] = both[4:8] - (lse[0:4] - lse[4:8])

    for r in range(2):
        others(*near_all(r)).wait_send()
        others(*far_all(r)).wait_send()
    for u in range(n_units):
        sent(u)
    for s in swaps + lent + sends:
        s.wait_send()


def finish(lt_ref, ld_ref, ex_ref, stat_ref, t_ref, d_ref, r_ref, accept_ref, left_ref, res, sem):
    copies = [pltpu.make_async_copy(lt_ref, t_ref, sem.at[0]), pltpu.make_async_copy(ld_ref, d_ref, sem.at[1])]
    for copy in copies:
        copy.start()
    left = stat_ref[0:4, :]
    left_ref[...] = left
    accept_ref[...] = jnp.exp(jnp.minimum(stat_ref[4:8, :], 0.0))
    scale = 1.0 / jnp.maximum(left, 0.25)
    for j in range(4):
        rows = slice(128 * j, 128 * j + 128)
        col = jnp.broadcast_to(scale[j : j + 1], (128, 128)).T
        for t in range(4):
            cols = slice(128 * t, 128 * t + 128)
            res[rows, cols] = ex_ref[rows, cols] * col
        copies.append(pltpu.make_async_copy(res.at[rows], r_ref.at[rows], sem.at[2 + j]))
        copies[-1].start()
    for copy in copies:
        copy.wait()


def on_device(target_hidden, target_weight, draft_hidden, draft_weight, draft_tokens):
    vmem, anywhere = pl.BlockSpec(memory_space=pltpu.VMEM), pl.BlockSpec(memory_space=pl.ANY)
    n_units = len(UNITS)
    dma = pltpu.SemaphoreType.DMA
    f32 = jnp.float32
    lt, ld, ex, stat = pl.pallas_call(
        kernel,
        name="verify",
        out_shape=(
            pltpu.VMEM((512, 512), f32),
            pltpu.VMEM((512, 512), f32),
            pltpu.VMEM((512, 512), f32),
            pltpu.VMEM((8, 128), f32),
        ),
        in_specs=[anywhere] * 5,
        out_specs=(vmem, vmem, vmem, vmem),
        scratch_shapes=(
            [pltpu.VMEM((2, 4, 4, 2, 16, size), jnp.bfloat16) for _, _, _, size in UNITS]
            + [pltpu.VMEM((2, 2, size, 512), jnp.bfloat16) for _, _, _, size in UNITS]
            + [
                pltpu.VMEM((4, 16384), jnp.bfloat16),
                pltpu.VMEM((4, 4096), jnp.bfloat16),
                pltpu.VMEM((4, 4, 4096), jnp.bfloat16),
                pltpu.VMEM((4, 4, 1024), jnp.bfloat16),
                pltpu.VMEM((2, 512, 512), f32),
                pltpu.VMEM((2, 512, 512), f32),
                pltpu.VMEM((512, 512), f32),
                pltpu.VMEM((512, 512), f32),
                pltpu.VMEM((4, 128), jnp.int32),
                pltpu.VMEM((4, 128), f32),
                pltpu.VMEM((8, 128), f32),
                pltpu.VMEM((2, 9, 8, 128), f32),
                pltpu.VMEM((2, 16, 8, 128), f32),
                dma((n_units,)), dma((n_units, 5)),
                dma((n_units,)), dma((n_units,)),
                dma((2, 4)), dma((2, 4)), dma((3,)),
                dma((2, 4)), dma((2, 4)),
                dma((2,)), dma((2,)),
                dma((2,)), dma((2,)),
            ]
        ),
        compiler_params=pltpu.CompilerParams(
            collective_id=0, has_side_effects=True, vmem_limit_bytes=48 * 2**20
        ),
    )(*[
        pltpu.with_memory_space_constraint(a, pltpu.HBM)
        for a in (
            target_hidden,
            target_weight.reshape(2, 2, 4096, 512),
            draft_hidden,
            draft_weight.reshape(2, 2, 1024, 512),
            draft_tokens.reshape(4, 128),
        )
    ])
    whole = jax.ShapeDtypeStruct((512, 512), f32)
    small = jax.ShapeDtypeStruct((4, 128), f32)
    held = [pltpu.with_memory_space_constraint(a, pltpu.VMEM) for a in (lt, ld, ex, stat)]
    t_log, d_log, residual, acceptance, leftover = pl.pallas_call(
        finish,
        name="finish",
        out_shape=(whole, whole, whole, small, small),
        in_specs=[vmem] * 4,
        out_specs=(anywhere, anywhere, anywhere, vmem, vmem),
        scratch_shapes=[pltpu.VMEM((512, 512), f32), dma((6,))],
        compiler_params=pltpu.CompilerParams(vmem_limit_bytes=8 * 2**20),
    )(*held)
    return t_log, d_log, residual, acceptance.reshape(512), leftover.reshape(512)


def solution(mesh):
    placed = (
        P(("wide", "narrow"), None),
        P(None, ("wide", "narrow")),
        P(("wide", "narrow"), None),
        P(None, ("wide", "narrow")),
        P(),
    )
    return jax.shard_map(
        on_device,
        mesh=mesh,
        in_specs=placed,
        out_specs=(
            P(None, ("wide", "narrow")),
            P(None, ("wide", "narrow")),
            P(None, ("wide", "narrow")),
            P(),
            P(),
        ),
        check_vma=False,
    )
```

```python
import functools

import jax
import jax.numpy as jnp
from jax import lax
from jax.experimental import pallas as pl
from jax.experimental.pallas import tpu as pltpu
from jax.sharding import PartitionSpec as P

MESH = pl.DeviceIdType.MESH
T = 128
ORDERS = (("x", "y", "z"), ("y", "z", "x"), ("z", "x", "y"))
SPLIT = (("d", (3, 3, 2)), ("t", (4, 4, 4)), ("t", (3, 3, 4)), ("t", (2, 2, 2)), ("t", (1, 1, 2)))


def make_units():
    units, used = [], {"d": 0, "t": 0}
    for kind, sizes in SPLIT:
        for order, size in enumerate(sizes):
            units.append((order, kind, used[kind] * T, size * T))
            used[kind] += size
    return units


UNITS = make_units()
GROUPS = len(SPLIT)


def view(sel):
    whole = slice(None)
    x = sel["x"]
    if x == "all":
        hi, lo = whole, whole
    elif isinstance(x, tuple):
        hi, lo = whole, x[1]
    else:
        hi, lo = lax.div(x, 2), lax.rem(x, 2)
    rest = []
    for name in ("y", "z"):
        v = sel[name]
        if isinstance(v, str):
            rest.append(whole)
        elif isinstance(v, tuple):
            rest.append(pl.ds(2 * v[1], 2))
        else:
            rest.append(v)
    return (lo, rest[0], rest[1], hi)


def kernel(ht_ref, wt_ref, hd_ref, wd_ref, tok_ref, lt_ref, ld_ref, ex_ref, stat_ref, *scratch):
    n_units = len(UNITS)
    hb = scratch[:n_units]
    wb = scratch[n_units : 2 * n_units]
    (hid_t, hid_d, stage_t, stage_d, acc_t, acc_d, part_t, part_d, tok_i, tok_f, tops, near, far,
     gs, gr, ws, wr, es, er, el, ps, pr, ns, nr, fs, fr) = scratch[2 * n_units :]
    w, n = lax.axis_index("wide"), lax.axis_index("narrow")
    pos = {"x": lax.div(n, 2) * 2 + lax.rem(w, 2), "y": lax.div(w, 8), "z": lax.rem(lax.div(w, 2), 4)}
    c = lax.rem(n, 2)

    def device(dx=0, dy=0, dz=0, dc=0):
        x = lax.rem(pos["x"] + dx, 4)
        y = lax.rem(pos["y"] + dy, 4)
        z = lax.rem(pos["z"] + dz, 4)
        return ((y * 4 + z) * 2 + lax.rem(x, 2), lax.div(x, 2) * 2 + lax.rem(c + dc, 2))

    def shift(dim, by):
        return device(**{"d" + dim: by})

    def remote(src, dst, send, recv, to):
        return pltpu.make_async_remote_copy(
            src_ref=src, dst_ref=dst, send_sem=send, recv_sem=recv, device_id=to, device_id_type=MESH
        )

    partner = device(dc=1)
    xh, xl = lax.div(pos["x"], 2), lax.rem(pos["x"], 2)
    me = xl * 2 + c

    got_t = pltpu.make_async_copy(ht_ref, hid_t, el.at[0])
    got_d = pltpu.make_async_copy(hd_ref, hid_d, el.at[1])
    got_tok = pltpu.make_async_copy(tok_ref, tok_i, el.at[2])
    got_d.start()
    got_t.start()
    got_tok.start()

    steps = (0, 1, 2, 1)
    near_offs = sorted(((a, b) for a in range(4) for b in range(2) if (a, b) != (0, 0)), key=lambda o: -2 * steps[o[0]] - o[1])
    far_offs = sorted(((a, b) for a in range(4) for b in range(4) if (a, b) != (0, 0)), key=lambda o: -steps[o[0]] - steps[o[1]])
    barrier = pltpu.get_barrier_semaphore()
    greeted = [device(**{"d" + d: by}) for by in (2, 1, 3) for d in "xyz"] + [partner, (w + 1 - 2 * xl, xh * 2 + 1 - c)]
    for to in greeted:
        pl.semaphore_signal(barrier, inc=1, device_id=to, device_id_type=MESH)
    for u, (order, kind, start, size) in enumerate(UNITS):
        ref = wt_ref if kind == "t" else wd_ref
        pltpu.make_async_copy(ref.at[c, :, pl.ds(start, size), :], wb[u].at[0], wr.at[u]).start()
    got_d.wait()
    got_t.wait()
    pl.semaphore_wait(barrier, len(greeted))

    swaps = []
    for j in range(1, 4):
        to = lax.rem(me + j, 4)
        to_c, to_l = lax.rem(to, 2), lax.div(to, 2)
        target = ((pos["y"] * 4 + pos["z"]) * 2 + to_l, xh * 2 + to_c)
        qt = pl.multiple_of(to_c * 8192 + to_l * 4096, T)
        qd = pl.multiple_of(to_c * 2048 + to_l * 1024, T)
        swaps.append(remote(hid_d.at[:, pl.ds(qd, 1024)], stage_d.at[me], es.at[1, j], er.at[1, j], target))
        swaps.append(remote(hid_t.at[:, pl.ds(qt, 4096)], stage_t.at[me], es.at[0, j], er.at[0, j], target))
    for s in swaps:
        s.start()
    own_t = pltpu.make_async_copy(
        hid_t.at[:, pl.ds(pl.multiple_of(c * 8192 + xl * 4096, T), 4096)], stage_t.at[me], el.at[0])
    own_d = pltpu.make_async_copy(
        hid_d.at[:, pl.ds(pl.multiple_of(c * 2048 + xl * 1024, T), 1024)], stage_d.at[me], el.at[1])
    own_t.start()
    own_d.start()
    lent = []
    for u, (order, kind, start, size) in enumerate(UNITS):
        ref = wt_ref if kind == "t" else wd_ref
        lent.append(remote(ref.at[1 - c, :, pl.ds(start, size), :], wb[u].at[1], ws.at[u], wr.at[u], partner))
        lent[-1].start()
    own_t.wait()
    own_d.wait()
    for s in swaps:
        s.wait_recv()

    sends = []

    def send(u, phase, src, to):
        remote(src, src, gs.at[u], gr.at[u, phase], to).start()

    def arrived(u, phase):
        got = (
            hb[u].at[0, 0, pl.ds(0, 3), 0],
            hb[u].at[0, 0],
            hb[u].at[0, 0, pl.ds(0, 2)],
            hb[u].at[0],
            hb[u].at[0, pl.ds(0, 2)],
        )[phase]
        remote(got, got, gs.at[u], gr.at[u, phase], partner).wait_recv()

    def sent(u):
        all63 = part_t.at[pl.ds(0, 504), pl.ds(0, UNITS[u][3])]
        remote(all63, all63, gs.at[u], gr.at[u, 0], partner).wait_send()

    def line(order, c2, part="all"):
        d1, d2, d3 = order
        return view({d1: part, d2: c2, d3: pos[d3]})

    def plane(order, c3, part="all"):
        d1, d2, d3 = order
        return view({d1: "all", d2: part, d3: c3})

    def up(dim):
        return lax.rem(pos[dim] + 1, 4)

    def down(dim):
        return lax.rem(pos[dim] + 3, 4)

    def phase1(u):
        o, kind, start, size = UNITS[u]
        order = ORDERS[o]
        stage = stage_t if kind == "t" else stage_d
        rows = [stage[j, :, start : start + size].astype(jnp.float32) for j in range(4)]
        hb[u][xl, pos["y"], pos["z"], xh] = jnp.concatenate(rows, axis=0).astype(jnp.bfloat16)
        mine = hb[u].at[xl, pos["y"], pos["z"], xh]
        for by in (2, 1, 3):
            send(u, 0, mine, shift(order[0], by))

    def phase2a(u):
        order = ORDERS[UNITS[u][0]]
        arrived(u, 0)
        mine = hb[u].at[line(order, pos[order[1]])]
        for by in (1, 3):
            send(u, 1, mine, shift(order[1], by))

    def phase2b(u):
        order = ORDERS[UNITS[u][0]]
        arrived(u, 1)
        d = order[1]
        send(u, 2, hb[u].at[line(order, down(d), ("half", 0))], shift(d, 1))
        send(u, 2, hb[u].at[line(order, up(d), ("half", 1))], shift(d, 3))

    def phase3a(u):
        order = ORDERS[UNITS[u][0]]
        arrived(u, 2)
        mine = hb[u].at[plane(order, pos[order[2]])]
        for by in (1, 3):
            send(u, 3, mine, shift(order[2], by))

    def phase3b(u):
        order = ORDERS[UNITS[u][0]]
        arrived(u, 3)
        d = order[2]
        send(u, 4, hb[u].at[plane(order, down(d), ("half", 0))], shift(d, 1))
        send(u, 4, hb[u].at[plane(order, up(d), ("half", 1))], shift(d, 3))

    begun = set()

    def multiply(u, sides=(1, 0), again=False):
        o, kind, start, size = UNITS[u]
        if not again:
            arrived(u, 4)
            remote(wb[u], wb[u], ws.at[u], wr.at[u], partner).wait_recv()
        acc = acc_t if kind == "t" else acc_d
        first = kind not in begun
        begun.add(kind)
        lhs = jnp.concatenate([hb[u][0].reshape(512, size), hb[u][1].reshape(512, size)], axis=1)
        for side in sides:
            for col in (0, 256):
                rhs = wb[u][side, :, :, col : col + 256].reshape(2 * size, 256)
                res = jnp.dot(lhs, rhs, preferred_element_type=jnp.float32)
                if first:
                    acc[side, :, col : col + 256] = res
                else:
                    acc[side, :, col : col + 256] += res

    def every(f, g):
        for u in range(3 * g, 3 * g + 3):
            f(u)

    def given(k, acc, part, j):
        rows = pl.ds(pl.multiple_of(j * 128, 128), 128)
        return remote(acc.at[1, rows, :], part.at[rows, :], ps.at[k, j], pr.at[k, j], partner)

    def give(k, acc, part):
        for j in range(4):
            sends.append(given(k, acc, part, j))
            sends[-1].start()

    def columns(row):
        return jnp.broadcast_to(row, (128, 128)).T

    def totals(k, acc, part, base):
        def body(j, carry):
            rows = pl.ds(pl.multiple_of(j * 128, 128), 128)
            given(k, acc, part, j).wait_recv()
            mixed = acc[0, rows, :] + part[rows, :]
            order = [32 * q + r for q in range(4) for r in (0, 16, 8, 24)]
            logits = jnp.concatenate([mixed[r : r + 8] for r in order], axis=0)
            acc[0, rows, :] = logits
            tiles = [logits[:, 128 * t : 128 * t + 128] for t in range(4)]
            most = jnp.maximum(jnp.maximum(tiles[0], tiles[1]), jnp.maximum(tiles[2], tiles[3]))
            top = jnp.max(most.T, axis=0, keepdims=True)
            top_col = columns(top)
            e = [jnp.exp(t - top_col) for t in tiles]
            part[rows, :] = jnp.concatenate(e, axis=1)
            tops[pl.ds(base + j, 1), :] = top
            total = jnp.sum(((e[0] + e[1]) + (e[2] + e[3])).T, axis=0, keepdims=True)
            near[0, 8, pl.ds(base + j, 1), :] = top + jnp.log(total)
            return carry

        lax.fori_loop(0, 4, body, 0)

    near_me = pos["x"] * 2 + c
    far_me = pos["y"] * 4 + pos["z"]

    def spread(buf, ss, rs, r, me, count, value, targets):
        buf[r, me] = value
        for to in targets:
            remote(buf.at[r, me], buf.at[r, me], ss.at[r], rs.at[r], to).start()

    def others(buf, ss, rs, r, count, targets):
        full = buf.at[r, pl.ds(0, count - 1)]
        return remote(full, full, ss.at[r], rs.at[r], targets[0])

    def gathered(buf, ss, rs, r, count, targets):
        others(buf, ss, rs, r, count, targets).wait_recv()
        return buf[r, 0:count]

    near_to = [device(dx=a, dc=b) for a, b in near_offs]
    far_to = [device(dy=a, dz=b) for a, b in far_offs]
    near_all = lambda r: (near, ns, nr, r, 8, near_to)
    far_all = lambda r: (far, fs, fr, r, 16, far_to)

    def merge(values):
        top = jnp.max(values, axis=0)
        return top + jnp.log(jnp.sum(jnp.exp(values - top[None]), axis=0))

    for phase in (phase1, phase2a, phase2b):
        for g in range(GROUPS):
            every(phase, g)
    every(phase3a, 0)
    every(phase3a, 1)
    every(phase3b, 0)
    every(phase3a, 2)
    every(phase3b, 1)
    every(phase3a, 3)
    every(multiply, 0)
    give(0, acc_d, part_d)
    every(phase3b, 2)
    every(phase3a, 4)
    every(multiply, 1)
    every(phase3b, 3)
    totals(0, acc_d, part_d, 4)
    every(phase3b, 4)
    every(multiply, 2)
    every(lambda u: multiply(u, (1,)), 3)
    every(lambda u: multiply(u, (1,)), 4)
    give(1, acc_t, part_t)
    every(lambda u: multiply(u, (0,), True), 3)
    every(lambda u: multiply(u, (0,), True), 4)
    totals(1, acc_t, part_t, 0)

    spread(near, ns, nr, 0, near_me, 8, near[0, 8], near_to)
    got_tok.wait()
    tok_f[...] = (tok_i[...] - (w * 4 + n) * 512).astype(jnp.float32)

    def pick(j, carry):
        rows = pl.ds(pl.multiple_of(j * 128, 128), 128)
        tok = columns(tok_f[pl.ds(j, 1), :])
        lanes = lax.broadcasted_iota(jnp.int32, (128, 128), 1).astype(jnp.float32)
        picked = None
        for t in range(4):
            cols = slice(128 * t, 128 * t + 128)
            p = jnp.where(tok == lanes + 128.0 * t, acc_t[0, rows, cols] - acc_d[0, rows, cols], 0.0)
            picked = p if picked is None else picked + p
        near[1, 8, pl.ds(4 + j, 1), :] = jnp.sum(picked.T, axis=0, keepdims=True)
        return carry

    lax.fori_loop(0, 4, pick, 0)
    lse = merge(gathered(*near_all(0)))
    spread(far, fs, fr, 0, far_me, 16, lse, far_to)
    lse = merge(gathered(*far_all(0)))
    near[0, 8] = lse
    tops[...] = jnp.exp(tops[...] - lse)

    def mass(j, carry):
        rows = pl.ds(pl.multiple_of(j * 128, 128), 128)
        t_col = columns(tops[pl.ds(j, 1), :])
        d_col = columns(tops[pl.ds(4 + j, 1), :])
        kept = None
        for t in range(4):
            cols = slice(128 * t, 128 * t + 128)
            e = jnp.maximum(part_t[rows, cols] * t_col - part_d[rows, cols] * d_col, 0.0)
            ex_ref[rows, cols] = e
            kept = e if kept is None else kept + e
        near[1, 8, pl.ds(j, 1), :] = jnp.sum(kept.T, axis=0, keepdims=True)
        return carry

    lax.fori_loop(0, 4, mass, 0)

    spread(near, ns, nr, 1, near_me, 8, near[1, 8], near_to)

    def normalize(j, carry):
        rows = pl.ds(pl.multiple_of(j * 128, 128), 128)
        t_col = columns(near[0, 8, pl.ds(j, 1), :])
        d_col = columns(near[0, 8, pl.ds(4 + j, 1), :])
        for t in range(4):
            cols = slice(128 * t, 128 * t + 128)
            lt_ref[rows, cols] = acc_t[0, rows, cols] - t_col
            ld_ref[rows, cols] = acc_d[0, rows, cols] - d_col
        return carry

    lax.fori_loop(0, 4, normalize, 0)
    both = jnp.sum(gathered(*near_all(1)), axis=0)
    spread(far, fs, fr, 1, far_me, 16, both, far_to)
    both = jnp.sum(gathered(*far_all(1)), axis=0)
    stat_ref[0:4, :] = both[0:4]
    stat_ref[4:8, :] = both[4:8] - (lse[0:4] - lse[4:8])

    for r in range(2):
        others(*near_all(r)).wait_send()
        others(*far_all(r)).wait_send()
    for u in range(n_units):
        sent(u)
    for s in swaps + lent + sends:
        s.wait_send()


def finish(lt_ref, ld_ref, ex_ref, stat_ref, t_ref, d_ref, r_ref, accept_ref, left_ref, res, sem):
    copies = [pltpu.make_async_copy(lt_ref, t_ref, sem.at[0]), pltpu.make_async_copy(ld_ref, d_ref, sem.at[1])]
    for copy in copies:
        copy.start()
    left = stat_ref[0:4, :]
    left_ref[...] = left
    accept_ref[...] = jnp.exp(jnp.minimum(stat_ref[4:8, :], 0.0))
    scale = 1.0 / jnp.maximum(left, 0.25)
    for j in range(4):
        rows = slice(128 * j, 128 * j + 128)
        col = jnp.broadcast_to(scale[j : j + 1], (128, 128)).T
        for t in range(4):
            cols = slice(128 * t, 128 * t + 128)
            res[rows, cols] = ex_ref[rows, cols] * col
        copies.append(pltpu.make_async_copy(res.at[rows], r_ref.at[rows], sem.at[2 + j]))
        copies[-1].start()
    for copy in copies:
        copy.wait()


def on_device(target_hidden, target_weight, draft_hidden, draft_weight, draft_tokens):
    vmem, anywhere = pl.BlockSpec(memory_space=pltpu.VMEM), pl.BlockSpec(memory_space=pl.ANY)
    n_units = len(UNITS)
    dma = pltpu.SemaphoreType.DMA
    f32 = jnp.float32
    lt, ld, ex, stat = pl.pallas_call(
        kernel,
        name="verify",
        out_shape=(
            pltpu.VMEM((512, 512), f32),
            pltpu.VMEM((512, 512), f32),
            pltpu.VMEM((512, 512), f32),
            pltpu.VMEM((8, 128), f32),
        ),
        in_specs=[anywhere] * 5,
        out_specs=(vmem, vmem, vmem, vmem),
        scratch_shapes=(
            [pltpu.VMEM((2, 4, 4, 2, 16, size), jnp.bfloat16) for _, _, _, size in UNITS]
            + [pltpu.VMEM((2, 2, size, 512), jnp.bfloat16) for _, _, _, size in UNITS]
            + [
                pltpu.VMEM((4, 16384), jnp.bfloat16),
                pltpu.VMEM((4, 4096), jnp.bfloat16),
                pltpu.VMEM((4, 4, 4096), jnp.bfloat16),
                pltpu.VMEM((4, 4, 1024), jnp.bfloat16),
                pltpu.VMEM((2, 512, 512), f32),
                pltpu.VMEM((2, 512, 512), f32),
                pltpu.VMEM((512, 512), f32),
                pltpu.VMEM((512, 512), f32),
                pltpu.VMEM((4, 128), jnp.int32),
                pltpu.VMEM((4, 128), f32),
                pltpu.VMEM((8, 128), f32),
                pltpu.VMEM((2, 9, 8, 128), f32),
                pltpu.VMEM((2, 16, 8, 128), f32),
                dma((n_units,)), dma((n_units, 5)),
                dma((n_units,)), dma((n_units,)),
                dma((2, 4)), dma((2, 4)), dma((3,)),
                dma((2, 4)), dma((2, 4)),
                dma((2,)), dma((2,)),
                dma((2,)), dma((2,)),
            ]
        ),
        compiler_params=pltpu.CompilerParams(
            collective_id=0, has_side_effects=True, vmem_limit_bytes=48 * 2**20
        ),
    )(*[
        pltpu.with_memory_space_constraint(a, pltpu.HBM)
        for a in (
            target_hidden,
            target_weight.reshape(2, 2, 4096, 512),
            draft_hidden,
            draft_weight.reshape(2, 2, 1024, 512),
            draft_tokens.reshape(4, 128),
        )
    ])
    whole = jax.ShapeDtypeStruct((512, 512), f32)
    small = jax.ShapeDtypeStruct((4, 128), f32)
    held = [pltpu.with_memory_space_constraint(a, pltpu.VMEM) for a in (lt, ld, ex, stat)]
    t_log, d_log, residual, acceptance, leftover = pl.pallas_call(
        finish,
        name="finish",
        out_shape=(whole, whole, whole, small, small),
        in_specs=[vmem] * 4,
        out_specs=(anywhere, anywhere, anywhere, vmem, vmem),
        scratch_shapes=[pltpu.VMEM((512, 512), f32), dma((6,))],
        compiler_params=pltpu.CompilerParams(vmem_limit_bytes=8 * 2**20),
    )(*held)
    return t_log, d_log, residual, acceptance.reshape(512), leftover.reshape(512)


def solution(mesh):
    placed = (
        P(("wide", "narrow"), None),
        P(None, ("wide", "narrow")),
        P(("wide", "narrow"), None),
        P(None, ("wide", "narrow")),
        P(),
    )
    return jax.shard_map(
        on_device,
        mesh=mesh,
        in_specs=placed,
        out_specs=(
            P(None, ("wide", "narrow")),
            P(None, ("wide", "narrow")),
            P(None, ("wide", "narrow")),
            P(),
            P(),
        ),
        check_vma=False,
    )
```

```python
import functools

import jax
import jax.numpy as jnp
from jax import lax
from jax.experimental import pallas as pl
from jax.experimental.pallas import tpu as pltpu
from jax.sharding import PartitionSpec as P

MESH = pl.DeviceIdType.MESH
T = 128
ORDERS = (("x", "y", "z"), ("y", "z", "x"), ("z", "x", "y"))
SPLIT = (("d", (3, 3, 2)), ("t", (4, 4, 4)), ("t", (3, 3, 4)), ("t", (2, 2, 2)), ("t", (1, 1, 2)))


def make_units():
    units, used = [], {"d": 0, "t": 0}
    for kind, sizes in SPLIT:
        for order, size in enumerate(sizes):
            units.append((order, kind, used[kind] * T, size * T))
            used[kind] += size
    return units


UNITS = make_units()
GROUPS = len(SPLIT)


def view(sel):
    whole = slice(None)
    x = sel["x"]
    if x == "all":
        hi, lo = whole, whole
    elif isinstance(x, tuple):
        hi, lo = whole, x[1]
    else:
        hi, lo = lax.div(x, 2), lax.rem(x, 2)
    rest = []
    for name in ("y", "z"):
        v = sel[name]
        if isinstance(v, str):
            rest.append(whole)
        elif isinstance(v, tuple):
            rest.append(pl.ds(2 * v[1], 2))
        else:
            rest.append(v)
    return (lo, rest[0], rest[1], hi)


def kernel(ht_ref, wt_ref, hd_ref, wd_ref, tok_ref, lt_ref, ld_ref, ex_ref, stat_ref, *scratch):
    n_units = len(UNITS)
    hb = scratch[:n_units]
    wb = scratch[n_units : 2 * n_units]
    (hid_t, hid_d, stage_t, stage_d, acc_t, acc_d, part_t, part_d, tok_i, tok_f, tops, near, far,
     gs, gr, ws, wr, es, er, el, ps, pr, ns, nr, fs, fr) = scratch[2 * n_units :]
    w, n = lax.axis_index("wide"), lax.axis_index("narrow")
    pos = {"x": lax.div(n, 2) * 2 + lax.rem(w, 2), "y": lax.div(w, 8), "z": lax.rem(lax.div(w, 2), 4)}
    c = lax.rem(n, 2)

    def device(dx=0, dy=0, dz=0, dc=0):
        x = lax.rem(pos["x"] + dx, 4)
        y = lax.rem(pos["y"] + dy, 4)
        z = lax.rem(pos["z"] + dz, 4)
        return ((y * 4 + z) * 2 + lax.rem(x, 2), lax.div(x, 2) * 2 + lax.rem(c + dc, 2))

    def shift(dim, by):
        return device(**{"d" + dim: by})

    def remote(src, dst, send, recv, to):
        return pltpu.make_async_remote_copy(
            src_ref=src, dst_ref=dst, send_sem=send, recv_sem=recv, device_id=to, device_id_type=MESH
        )

    partner = device(dc=1)
    xh, xl = lax.div(pos["x"], 2), lax.rem(pos["x"], 2)
    me = xl * 2 + c

    got_t = pltpu.make_async_copy(ht_ref, hid_t, el.at[0])
    got_d = pltpu.make_async_copy(hd_ref, hid_d, el.at[1])
    got_tok = pltpu.make_async_copy(tok_ref, tok_i, el.at[2])
    got_d.start()
    got_t.start()
    got_tok.start()

    steps = (0, 1, 2, 1)
    near_offs = sorted(((a, b) for a in range(4) for b in range(2) if (a, b) != (0, 0)), key=lambda o: -2 * steps[o[0]] - o[1])
    far_offs = sorted(((a, b) for a in range(4) for b in range(4) if (a, b) != (0, 0)), key=lambda o: -steps[o[0]] - steps[o[1]])
    barrier = pltpu.get_barrier_semaphore()
    greeted = [device(**{"d" + d: by}) for by in (2, 1, 3) for d in "xyz"] + [partner, (w + 1 - 2 * xl, xh * 2 + 1 - c)]
    for to in greeted:
        pl.semaphore_signal(barrier, inc=1, device_id=to, device_id_type=MESH)
    for u, (order, kind, start, size) in enumerate(UNITS):
        ref = wt_ref if kind == "t" else wd_ref
        pltpu.make_async_copy(ref.at[c, :, pl.ds(start, size), :], wb[u].at[0], wr.at[u]).start()
    got_d.wait()
    got_t.wait()
    pl.semaphore_wait(barrier, len(greeted))

    swaps = []
    for j in range(1, 4):
        to = lax.rem(me + j, 4)
        to_c, to_l = lax.rem(to, 2), lax.div(to, 2)
        target = ((pos["y"] * 4 + pos["z"]) * 2 + to_l, xh * 2 + to_c)
        qt = pl.multiple_of(to_c * 8192 + to_l * 4096, T)
        qd = pl.multiple_of(to_c * 2048 + to_l * 1024, T)
        swaps.insert(j - 1, remote(hid_d.at[:, pl.ds(qd, 1024)], stage_d.at[me], es.at[1, j], er.at[1, j], target))
        swaps.append(remote(hid_t.at[:, pl.ds(qt, 4096)], stage_t.at[me], es.at[0, j], er.at[0, j], target))
    for s in swaps:
        s.start()
    own_t = pltpu.make_async_copy(
        hid_t.at[:, pl.ds(pl.multiple_of(c * 8192 + xl * 4096, T), 4096)], stage_t.at[me], el.at[0])
    own_d = pltpu.make_async_copy(
        hid_d.at[:, pl.ds(pl.multiple_of(c * 2048 + xl * 1024, T), 1024)], stage_d.at[me], el.at[1])
    own_t.start()
    own_d.start()
    lent = []
    for u, (order, kind, start, size) in enumerate(UNITS):
        ref = wt_ref if kind == "t" else wd_ref
        lent.append(remote(ref.at[1 - c, :, pl.ds(start, size), :], wb[u].at[1], ws.at[u], wr.at[u], partner))
        lent[-1].start()
    swaps_d, swaps_t = swaps[:3], swaps[3:]

    sends = []

    def send(u, phase, src, to):
        remote(src, src, gs.at[u], gr.at[u, phase], to).start()

    def arrived(u, phase):
        got = (
            hb[u].at[0, 0, pl.ds(0, 3), 0],
            hb[u].at[0, 0],
            hb[u].at[0, 0, pl.ds(0, 2)],
            hb[u].at[0],
            hb[u].at[0, pl.ds(0, 2)],
        )[phase]
        remote(got, got, gs.at[u], gr.at[u, phase], partner).wait_recv()

    def sent(u):
        all63 = part_t.at[pl.ds(0, 504), pl.ds(0, UNITS[u][3])]
        remote(all63, all63, gs.at[u], gr.at[u, 0], partner).wait_send()

    def line(order, c2, part="all"):
        d1, d2, d3 = order
        return view({d1: part, d2: c2, d3: pos[d3]})

    def plane(order, c3, part="all"):
        d1, d2, d3 = order
        return view({d1: "all", d2: part, d3: c3})

    def up(dim):
        return lax.rem(pos[dim] + 1, 4)

    def down(dim):
        return lax.rem(pos[dim] + 3, 4)

    def phase1(u):
        o, kind, start, size = UNITS[u]
        order = ORDERS[o]
        stage = stage_t if kind == "t" else stage_d
        rows = [stage[j, :, start : start + size].astype(jnp.float32) for j in range(4)]
        hb[u][xl, pos["y"], pos["z"], xh] = jnp.concatenate(rows, axis=0).astype(jnp.bfloat16)
        mine = hb[u].at[xl, pos["y"], pos["z"], xh]
        for by in (2, 1, 3):
            send(u, 0, mine, shift(order[0], by))

    def phase2a(u):
        order = ORDERS[UNITS[u][0]]
        arrived(u, 0)
        mine = hb[u].at[line(order, pos[order[1]])]
        for by in (1, 3):
            send(u, 1, mine, shift(order[1], by))

    def phase2b(u):
        order = ORDERS[UNITS[u][0]]
        arrived(u, 1)
        d = order[1]
        send(u, 2, hb[u].at[line(order, down(d), ("half", 0))], shift(d, 1))
        send(u, 2, hb[u].at[line(order, up(d), ("half", 1))], shift(d, 3))

    def phase3a(u):
        order = ORDERS[UNITS[u][0]]
        arrived(u, 2)
        mine = hb[u].at[plane(order, pos[order[2]])]
        for by in (1, 3):
            send(u, 3, mine, shift(order[2], by))

    def phase3b(u):
        order = ORDERS[UNITS[u][0]]
        arrived(u, 3)
        d = order[2]
        send(u, 4, hb[u].at[plane(order, down(d), ("half", 0))], shift(d, 1))
        send(u, 4, hb[u].at[plane(order, up(d), ("half", 1))], shift(d, 3))

    begun = set()

    def multiply(u, sides=(1, 0), again=False):
        o, kind, start, size = UNITS[u]
        if not again:
            arrived(u, 4)
            remote(wb[u], wb[u], ws.at[u], wr.at[u], partner).wait_recv()
        acc = acc_t if kind == "t" else acc_d
        first = kind not in begun
        begun.add(kind)
        lhs = jnp.concatenate([hb[u][0].reshape(512, size), hb[u][1].reshape(512, size)], axis=1)
        for side in sides:
            for col in (0, 256):
                rhs = wb[u][side, :, :, col : col + 256].reshape(2 * size, 256)
                res = jnp.dot(lhs, rhs, preferred_element_type=jnp.float32)
                if first:
                    acc[side, :, col : col + 256] = res
                else:
                    acc[side, :, col : col + 256] += res

    def every(f, g):
        for u in range(3 * g, 3 * g + 3):
            f(u)

    def given(k, acc, part, j):
        rows = pl.ds(pl.multiple_of(j * 128, 128), 128)
        return remote(acc.at[1, rows, :], part.at[rows, :], ps.at[k, j], pr.at[k, j], partner)

    def give(k, acc, part):
        for j in range(4):
            sends.append(given(k, acc, part, j))
            sends[-1].start()

    def columns(row):
        return jnp.broadcast_to(row, (128, 128)).T

    def totals(k, acc, part, base):
        def body(j, carry):
            rows = pl.ds(pl.multiple_of(j * 128, 128), 128)
            given(k, acc, part, j).wait_recv()
            mixed = acc[0, rows, :] + part[rows, :]
            order = [32 * q + r for q in range(4) for r in (0, 16, 8, 24)]
            logits = jnp.concatenate([mixed[r : r + 8] for r in order], axis=0)
            acc[0, rows, :] = logits
            tiles = [logits[:, 128 * t : 128 * t + 128] for t in range(4)]
            most = jnp.maximum(jnp.maximum(tiles[0], tiles[1]), jnp.maximum(tiles[2], tiles[3]))
            top = jnp.max(most.T, axis=0, keepdims=True)
            top_col = columns(top)
            e = [jnp.exp(t - top_col) for t in tiles]
            part[rows, :] = jnp.concatenate(e, axis=1)
            tops[pl.ds(base + j, 1), :] = top
            total = jnp.sum(((e[0] + e[1]) + (e[2] + e[3])).T, axis=0, keepdims=True)
            near[0, 8, pl.ds(base + j, 1), :] = top + jnp.log(total)
            return carry

        lax.fori_loop(0, 4, body, 0)

    near_me = pos["x"] * 2 + c
    far_me = pos["y"] * 4 + pos["z"]

    def spread(buf, ss, rs, r, me, count, value, targets):
        buf[r, me] = value
        for to in targets:
            remote(buf.at[r, me], buf.at[r, me], ss.at[r], rs.at[r], to).start()

    def others(buf, ss, rs, r, count, targets):
        full = buf.at[r, pl.ds(0, count - 1)]
        return remote(full, full, ss.at[r], rs.at[r], targets[0])

    def gathered(buf, ss, rs, r, count, targets):
        others(buf, ss, rs, r, count, targets).wait_recv()
        return buf[r, 0:count]

    near_to = [device(dx=a, dc=b) for a, b in near_offs]
    far_to = [device(dy=a, dz=b) for a, b in far_offs]
    near_all = lambda r: (near, ns, nr, r, 8, near_to)
    far_all = lambda r: (far, fs, fr, r, 16, far_to)

    def merge(values):
        top = jnp.max(values, axis=0)
        return top + jnp.log(jnp.sum(jnp.exp(values - top[None]), axis=0))

    own_d.wait()
    for s in swaps_d:
        s.wait_recv()
    every(phase1, 0)
    own_t.wait()
    for s in swaps_t:
        s.wait_recv()
    for g in range(1, GROUPS):
        every(phase1, g)
    for phase in (phase2a, phase2b):
        for g in range(GROUPS):
            every(phase, g)
    every(phase3a, 0)
    every(phase3a, 1)
    every(phase3b, 0)
    every(phase3a, 2)
    every(phase3b, 1)
    every(phase3a, 3)
    every(multiply, 0)
    give(0, acc_d, part_d)
    every(phase3b, 2)
    every(phase3a, 4)
    every(multiply, 1)
    every(phase3b, 3)
    totals(0, acc_d, part_d, 4)
    every(phase3b, 4)
    every(multiply, 2)
    every(lambda u: multiply(u, (1,)), 3)
    every(lambda u: multiply(u, (1,)), 4)
    give(1, acc_t, part_t)
    every(lambda u: multiply(u, (0,), True), 3)
    every(lambda u: multiply(u, (0,), True), 4)
    totals(1, acc_t, part_t, 0)

    spread(near, ns, nr, 0, near_me, 8, near[0, 8], near_to)
    got_tok.wait()
    tok_f[...] = (tok_i[...] - (w * 4 + n) * 512).astype(jnp.float32)

    def pick(j, carry):
        rows = pl.ds(pl.multiple_of(j * 128, 128), 128)
        tok = columns(tok_f[pl.ds(j, 1), :])
        lanes = lax.broadcasted_iota(jnp.int32, (128, 128), 1).astype(jnp.float32)
        picked = None
        for t in range(4):
            cols = slice(128 * t, 128 * t + 128)
            p = jnp.where(tok == lanes + 128.0 * t, acc_t[0, rows, cols] - acc_d[0, rows, cols], 0.0)
            picked = p if picked is None else picked + p
        near[1, 8, pl.ds(4 + j, 1), :] = jnp.sum(picked.T, axis=0, keepdims=True)
        return carry

    lax.fori_loop(0, 4, pick, 0)
    lse = merge(gathered(*near_all(0)))
    spread(far, fs, fr, 0, far_me, 16, lse, far_to)
    lse = merge(gathered(*far_all(0)))
    near[0, 8] = lse
    tops[...] = jnp.exp(tops[...] - lse)

    def mass(j, carry):
        rows = pl.ds(pl.multiple_of(j * 128, 128), 128)
        t_col = columns(tops[pl.ds(j, 1), :])
        d_col = columns(tops[pl.ds(4 + j, 1), :])
        kept = None
        for t in range(4):
            cols = slice(128 * t, 128 * t + 128)
            e = jnp.maximum(part_t[rows, cols] * t_col - part_d[rows, cols] * d_col, 0.0)
            ex_ref[rows, cols] = e
            kept = e if kept is None else kept + e
        near[1, 8, pl.ds(j, 1), :] = jnp.sum(kept.T, axis=0, keepdims=True)
        return carry

    lax.fori_loop(0, 4, mass, 0)

    spread(near, ns, nr, 1, near_me, 8, near[1, 8], near_to)

    def normalize(j, carry):
        rows = pl.ds(pl.multiple_of(j * 128, 128), 128)
        t_col = columns(near[0, 8, pl.ds(j, 1), :])
        d_col = columns(near[0, 8, pl.ds(4 + j, 1), :])
        for t in range(4):
            cols = slice(128 * t, 128 * t + 128)
            lt_ref[rows, cols] = acc_t[0, rows, cols] - t_col
            ld_ref[rows, cols] = acc_d[0, rows, cols] - d_col
        return carry

    lax.fori_loop(0, 4, normalize, 0)
    for u in range(n_units):
        sent(u)
    for s in swaps + lent + sends:
        s.wait_send()
    others(*near_all(0)).wait_send()
    others(*far_all(0)).wait_send()
    both = jnp.sum(gathered(*near_all(1)), axis=0)
    spread(far, fs, fr, 1, far_me, 16, both, far_to)
    both = jnp.sum(gathered(*far_all(1)), axis=0)
    stat_ref[0:4, :] = both[0:4]
    stat_ref[4:8, :] = both[4:8] - (lse[0:4] - lse[4:8])

    others(*near_all(1)).wait_send()
    others(*far_all(1)).wait_send()


def finish(lt_ref, ld_ref, ex_ref, stat_ref, t_ref, d_ref, r_ref, accept_ref, left_ref, res, sem):
    copies = [pltpu.make_async_copy(lt_ref, t_ref, sem.at[0]), pltpu.make_async_copy(ld_ref, d_ref, sem.at[1])]
    for copy in copies:
        copy.start()
    left = stat_ref[0:4, :]
    left_ref[...] = left
    accept_ref[...] = jnp.exp(jnp.minimum(stat_ref[4:8, :], 0.0))
    scale = 1.0 / jnp.maximum(left, 0.25)
    for j in range(4):
        rows = slice(128 * j, 128 * j + 128)
        col = jnp.broadcast_to(scale[j : j + 1], (128, 128)).T
        for t in range(4):
            cols = slice(128 * t, 128 * t + 128)
            res[rows, cols] = ex_ref[rows, cols] * col
        copies.append(pltpu.make_async_copy(res.at[rows], r_ref.at[rows], sem.at[2 + j]))
        copies[-1].start()
    for copy in copies:
        copy.wait()


def on_device(target_hidden, target_weight, draft_hidden, draft_weight, draft_tokens):
    vmem, anywhere = pl.BlockSpec(memory_space=pltpu.VMEM), pl.BlockSpec(memory_space=pl.ANY)
    n_units = len(UNITS)
    dma = pltpu.SemaphoreType.DMA
    f32 = jnp.float32
    lt, ld, ex, stat = pl.pallas_call(
        kernel,
        name="verify",
        out_shape=(
            pltpu.VMEM((512, 512), f32),
            pltpu.VMEM((512, 512), f32),
            pltpu.VMEM((512, 512), f32),
            pltpu.VMEM((8, 128), f32),
        ),
        in_specs=[anywhere] * 5,
        out_specs=(vmem, vmem, vmem, vmem),
        scratch_shapes=(
            [pltpu.VMEM((2, 4, 4, 2, 16, size), jnp.bfloat16) for _, _, _, size in UNITS]
            + [pltpu.VMEM((2, 2, size, 512), jnp.bfloat16) for _, _, _, size in UNITS]
            + [
                pltpu.VMEM((4, 16384), jnp.bfloat16),
                pltpu.VMEM((4, 4096), jnp.bfloat16),
                pltpu.VMEM((4, 4, 4096), jnp.bfloat16),
                pltpu.VMEM((4, 4, 1024), jnp.bfloat16),
                pltpu.VMEM((2, 512, 512), f32),
                pltpu.VMEM((2, 512, 512), f32),
                pltpu.VMEM((512, 512), f32),
                pltpu.VMEM((512, 512), f32),
                pltpu.VMEM((4, 128), jnp.int32),
                pltpu.VMEM((4, 128), f32),
                pltpu.VMEM((8, 128), f32),
                pltpu.VMEM((2, 9, 8, 128), f32),
                pltpu.VMEM((2, 16, 8, 128), f32),
                dma((n_units,)), dma((n_units, 5)),
                dma((n_units,)), dma((n_units,)),
                dma((2, 4)), dma((2, 4)), dma((3,)),
                dma((2, 4)), dma((2, 4)),
                dma((2,)), dma((2,)),
                dma((2,)), dma((2,)),
            ]
        ),
        compiler_params=pltpu.CompilerParams(
            collective_id=0, has_side_effects=True, vmem_limit_bytes=48 * 2**20
        ),
    )(*[
        pltpu.with_memory_space_constraint(a, pltpu.HBM)
        for a in (
            target_hidden,
            target_weight.reshape(2, 2, 4096, 512),
            draft_hidden,
            draft_weight.reshape(2, 2, 1024, 512),
            draft_tokens.reshape(4, 128),
        )
    ])
    whole = jax.ShapeDtypeStruct((512, 512), f32)
    small = jax.ShapeDtypeStruct((4, 128), f32)
    held = [pltpu.with_memory_space_constraint(a, pltpu.VMEM) for a in (lt, ld, ex, stat)]
    t_log, d_log, residual, acceptance, leftover = pl.pallas_call(
        finish,
        name="finish",
        out_shape=(whole, whole, whole, small, small),
        in_specs=[vmem] * 4,
        out_specs=(anywhere, anywhere, anywhere, vmem, vmem),
        scratch_shapes=[pltpu.VMEM((512, 512), f32), dma((6,))],
        compiler_params=pltpu.CompilerParams(vmem_limit_bytes=8 * 2**20),
    )(*held)
    return t_log, d_log, residual, acceptance.reshape(512), leftover.reshape(512)


def solution(mesh):
    placed = (
        P(("wide", "narrow"), None),
        P(None, ("wide", "narrow")),
        P(("wide", "narrow"), None),
        P(None, ("wide", "narrow")),
        P(),
    )
    return jax.shard_map(
        on_device,
        mesh=mesh,
        in_specs=placed,
        out_specs=(
            P(None, ("wide", "narrow")),
            P(None, ("wide", "narrow")),
            P(None, ("wide", "narrow")),
            P(),
            P(),
        ),
        check_vma=False,
    )
```

```python
import functools

import jax
import jax.numpy as jnp
from jax import lax
from jax.experimental import pallas as pl
from jax.experimental.pallas import tpu as pltpu
from jax.sharding import PartitionSpec as P

MESH = pl.DeviceIdType.MESH
T = 128
ORDERS = (("x", "y", "z"), ("y", "z", "x"), ("z", "x", "y"))
SPLIT = (("d", (3, 3, 2)), ("t", (4, 4, 4)), ("t", (3, 3, 4)), ("t", (2, 2, 2)), ("t", (1, 1, 2)))


def make_units():
    units, used = [], {"d": 0, "t": 0}
    for kind, sizes in SPLIT:
        for order, size in enumerate(sizes):
            units.append((order, kind, used[kind] * T, size * T))
            used[kind] += size
    return units


UNITS = make_units()
GROUPS = len(SPLIT)


def view(sel):
    whole = slice(None)
    x = sel["x"]
    if x == "all":
        hi, lo = whole, whole
    elif isinstance(x, tuple):
        hi, lo = whole, x[1]
    else:
        hi, lo = lax.div(x, 2), lax.rem(x, 2)
    rest = []
    for name in ("y", "z"):
        v = sel[name]
        if isinstance(v, str):
            rest.append(whole)
        elif isinstance(v, tuple):
            rest.append(pl.ds(2 * v[1], 2))
        else:
            rest.append(v)
    return (lo, rest[0], rest[1], hi)


def kernel(ht_ref, wt_ref, hd_ref, wd_ref, tok_ref, lt_ref, ld_ref, ex_ref, stat_ref, *scratch):
    n_units = len(UNITS)
    hb = scratch[:n_units]
    wb = scratch[n_units : 2 * n_units]
    (hid_t, hid_d, stage_t, stage_d, acc_t, acc_d, part_t, part_d, tok_i, tok_f, tops, near, far,
     gs, gr, ws, wr, es, er, el, ps, pr, ns, nr, fs, fr) = scratch[2 * n_units :]
    w, n = lax.axis_index("wide"), lax.axis_index("narrow")
    pos = {"x": lax.div(n, 2) * 2 + lax.rem(w, 2), "y": lax.div(w, 8), "z": lax.rem(lax.div(w, 2), 4)}
    c = lax.rem(n, 2)

    def device(dx=0, dy=0, dz=0, dc=0):
        x = lax.rem(pos["x"] + dx, 4)
        y = lax.rem(pos["y"] + dy, 4)
        z = lax.rem(pos["z"] + dz, 4)
        return ((y * 4 + z) * 2 + lax.rem(x, 2), lax.div(x, 2) * 2 + lax.rem(c + dc, 2))

    def shift(dim, by):
        return device(**{"d" + dim: by})

    def remote(src, dst, send, recv, to):
        return pltpu.make_async_remote_copy(
            src_ref=src, dst_ref=dst, send_sem=send, recv_sem=recv, device_id=to, device_id_type=MESH
        )

    partner = device(dc=1)
    xh, xl = lax.div(pos["x"], 2), lax.rem(pos["x"], 2)
    me = xl * 2 + c

    got_t = pltpu.make_async_copy(ht_ref, hid_t, el.at[0])
    got_d = pltpu.make_async_copy(hd_ref, hid_d, el.at[1])
    got_tok = pltpu.make_async_copy(tok_ref, tok_i, el.at[2])
    got_d.start()
    got_t.start()
    got_tok.start()

    steps = (0, 1, 2, 1)
    near_offs = sorted(((a, b) for a in range(4) for b in range(2) if (a, b) != (0, 0)), key=lambda o: -2 * steps[o[0]] - o[1])
    far_offs = sorted(((a, b) for a in range(4) for b in range(4) if (a, b) != (0, 0)), key=lambda o: -steps[o[0]] - steps[o[1]])
    barrier = pltpu.get_barrier_semaphore()
    greeted = [device(**{"d" + d: by}) for by in (2, 1, 3) for d in "xyz"] + [partner, (w + 1 - 2 * xl, xh * 2 + 1 - c)]
    for to in greeted:
        pl.semaphore_signal(barrier, inc=1, device_id=to, device_id_type=MESH)
    for u, (order, kind, start, size) in enumerate(UNITS):
        ref = wt_ref if kind == "t" else wd_ref
        pltpu.make_async_copy(ref.at[c, :, pl.ds(start, size), :], wb[u].at[0], wr.at[u]).start()
    got_d.wait()
    got_t.wait()
    pl.semaphore_wait(barrier, len(greeted))

    swaps = []
    for j in range(1, 4):
        to = lax.rem(me + j, 4)
        to_c, to_l = lax.rem(to, 2), lax.div(to, 2)
        target = ((pos["y"] * 4 + pos["z"]) * 2 + to_l, xh * 2 + to_c)
        qt = pl.multiple_of(to_c * 8192 + to_l * 4096, T)
        qd = pl.multiple_of(to_c * 2048 + to_l * 1024, T)
        swaps.insert(j - 1, remote(hid_d.at[:, pl.ds(qd, 1024)], stage_d.at[me], es.at[1, j], er.at[1, j], target))
        swaps.append(remote(hid_t.at[:, pl.ds(qt, 4096)], stage_t.at[me], es.at[0, j], er.at[0, j], target))
    for s in swaps:
        s.start()
    own_t = pltpu.make_async_copy(
        hid_t.at[:, pl.ds(pl.multiple_of(c * 8192 + xl * 4096, T), 4096)], stage_t.at[me], el.at[0])
    own_d = pltpu.make_async_copy(
        hid_d.at[:, pl.ds(pl.multiple_of(c * 2048 + xl * 1024, T), 1024)], stage_d.at[me], el.at[1])
    own_t.start()
    own_d.start()
    lent = []
    for u, (order, kind, start, size) in enumerate(UNITS):
        ref = wt_ref if kind == "t" else wd_ref
        lent.append(remote(ref.at[1 - c, :, pl.ds(start, size), :], wb[u].at[1], ws.at[u], wr.at[u], partner))
        lent[-1].start()
    swaps_d, swaps_t = swaps[:3], swaps[3:]

    sends = []

    def send(u, phase, src, to):
        remote(src, src, gs.at[u], gr.at[u, phase], to).start()

    def arrived(u, phase):
        got = (
            hb[u].at[0, 0, pl.ds(0, 3), 0],
            hb[u].at[0, 0],
            hb[u].at[0, 0, pl.ds(0, 2)],
            hb[u].at[0],
            hb[u].at[0, pl.ds(0, 2)],
        )[phase]
        remote(got, got, gs.at[u], gr.at[u, phase], partner).wait_recv()

    def sent(u):
        all63 = part_t.at[pl.ds(0, 504), pl.ds(0, UNITS[u][3])]
        remote(all63, all63, gs.at[u], gr.at[u, 0], partner).wait_send()

    def line(order, c2, part="all"):
        d1, d2, d3 = order
        return view({d1: part, d2: c2, d3: pos[d3]})

    def plane(order, c3, part="all"):
        d1, d2, d3 = order
        return view({d1: "all", d2: part, d3: c3})

    def up(dim):
        return lax.rem(pos[dim] + 1, 4)

    def down(dim):
        return lax.rem(pos[dim] + 3, 4)

    def phase1(u):
        o, kind, start, size = UNITS[u]
        order = ORDERS[o]
        stage = stage_t if kind == "t" else stage_d
        rows = [stage[j, :, start : start + size].astype(jnp.float32) for j in range(4)]
        hb[u][xl, pos["y"], pos["z"], xh] = jnp.concatenate(rows, axis=0).astype(jnp.bfloat16)
        mine = hb[u].at[xl, pos["y"], pos["z"], xh]
        for by in (2, 1, 3):
            send(u, 0, mine, shift(order[0], by))

    def phase2a(u):
        order = ORDERS[UNITS[u][0]]
        arrived(u, 0)
        mine = hb[u].at[line(order, pos[order[1]])]
        for by in (1, 3):
            send(u, 1, mine, shift(order[1], by))

    def phase2b(u):
        order = ORDERS[UNITS[u][0]]
        arrived(u, 1)
        d = order[1]
        send(u, 2, hb[u].at[line(order, down(d), ("half", 0))], shift(d, 1))
        send(u, 2, hb[u].at[line(order, up(d), ("half", 1))], shift(d, 3))

    def phase3a(u):
        order = ORDERS[UNITS[u][0]]
        arrived(u, 2)
        mine = hb[u].at[plane(order, pos[order[2]])]
        for by in (1, 3):
            send(u, 3, mine, shift(order[2], by))

    def phase3b(u):
        order = ORDERS[UNITS[u][0]]
        arrived(u, 3)
        d = order[2]
        send(u, 4, hb[u].at[plane(order, down(d), ("half", 0))], shift(d, 1))
        send(u, 4, hb[u].at[plane(order, up(d), ("half", 1))], shift(d, 3))

    begun = set()

    def multiply(u, sides=(1, 0), again=False):
        o, kind, start, size = UNITS[u]
        if not again:
            arrived(u, 4)
            remote(wb[u], wb[u], ws.at[u], wr.at[u], partner).wait_recv()
        acc = acc_t if kind == "t" else acc_d
        first = kind not in begun
        begun.add(kind)
        lhs = jnp.concatenate([hb[u][0].reshape(512, size), hb[u][1].reshape(512, size)], axis=1)
        for side in sides:
            for col in (0, 256):
                rhs = wb[u][side, :, :, col : col + 256].reshape(2 * size, 256)
                res = jnp.dot(lhs, rhs, preferred_element_type=jnp.float32)
                if first:
                    acc[side, :, col : col + 256] = res
                else:
                    acc[side, :, col : col + 256] += res

    def every(f, g):
        for u in range(3 * g, 3 * g + 3):
            f(u)

    def given(k, acc, part, j):
        rows = pl.ds(pl.multiple_of(j * 128, 128), 128)
        return remote(acc.at[1, rows, :], part.at[rows, :], ps.at[k, j], pr.at[k, j], partner)

    def give(k, acc, part):
        for j in range(4):
            sends.append(given(k, acc, part, j))
            sends[-1].start()

    def columns(row):
        return jnp.broadcast_to(row, (128, 128)).T

    def totals(k, acc, part, base):
        def body(j, carry):
            rows = pl.ds(pl.multiple_of(j * 128, 128), 128)
            given(k, acc, part, j).wait_recv()
            mixed = acc[0, rows, :] + part[rows, :]
            order = [32 * q + r for q in range(4) for r in (0, 16, 8, 24)]
            logits = jnp.concatenate([mixed[r : r + 8] for r in order], axis=0)
            acc[0, rows, :] = logits
            tiles = [logits[:, 128 * t : 128 * t + 128] for t in range(4)]
            most = jnp.maximum(jnp.maximum(tiles[0], tiles[1]), jnp.maximum(tiles[2], tiles[3]))
            top = jnp.max(most.T, axis=0, keepdims=True)
            top_col = columns(top)
            e = [jnp.exp(t - top_col) for t in tiles]
            part[rows, :] = jnp.concatenate(e, axis=1)
            tops[pl.ds(base + j, 1), :] = top
            total = jnp.sum(((e[0] + e[1]) + (e[2] + e[3])).T, axis=0, keepdims=True)
            near[0, 8, pl.ds(base + j, 1), :] = top + jnp.log(total)
            return carry

        lax.fori_loop(0, 4, body, 0)

    near_me = pos["x"] * 2 + c
    far_me = pos["y"] * 4 + pos["z"]

    def spread(buf, ss, rs, r, me, count, value, targets):
        buf[r, me] = value
        for to in targets:
            remote(buf.at[r, me], buf.at[r, me], ss.at[r], rs.at[r], to).start()

    def others(buf, ss, rs, r, count, targets):
        full = buf.at[r, pl.ds(0, count - 1)]
        return remote(full, full, ss.at[r], rs.at[r], targets[0])

    def gathered(buf, ss, rs, r, count, targets):
        others(buf, ss, rs, r, count, targets).wait_recv()
        return buf[r, 0:count]

    near_to = [device(dx=a, dc=b) for a, b in near_offs]
    far_to = [device(dy=a, dz=b) for a, b in far_offs]
    near_all = lambda r: (near, ns, nr, r, 8, near_to)
    far_all = lambda r: (far, fs, fr, r, 16, far_to)

    def merge(values):
        top = jnp.max(values, axis=0)
        return top + jnp.log(jnp.sum(jnp.exp(values - top[None]), axis=0))

    own_d.wait()
    for s in swaps_d:
        s.wait_recv()
    every(phase1, 0)
    own_t.wait()
    for s in swaps_t:
        s.wait_recv()
    for g in range(1, GROUPS):
        every(phase1, g)
    for phase in (phase2a, phase2b):
        for g in range(GROUPS):
            every(phase, g)
    every(phase3a, 0)
    every(phase3a, 1)
    every(phase3b, 0)
    every(phase3a, 2)
    every(phase3b, 1)
    every(phase3a, 3)
    every(multiply, 0)
    give(0, acc_d, part_d)
    every(phase3b, 2)
    every(phase3a, 4)
    multiply(3)
    multiply(4)
    every(phase3b, 3)
    multiply(5)
    totals(0, acc_d, part_d, 4)
    multiply(6)
    every(phase3b, 4)
    multiply(7)
    multiply(8)
    every(lambda u: multiply(u, (1,)), 3)
    every(lambda u: multiply(u, (1,)), 4)
    give(1, acc_t, part_t)
    every(lambda u: multiply(u, (0,), True), 3)
    every(lambda u: multiply(u, (0,), True), 4)
    totals(1, acc_t, part_t, 0)

    spread(near, ns, nr, 0, near_me, 8, near[0, 8], near_to)
    got_tok.wait()
    tok_f[...] = (tok_i[...] - (w * 4 + n) * 512).astype(jnp.float32)

    def pick(j, carry):
        rows = pl.ds(pl.multiple_of(j * 128, 128), 128)
        tok = columns(tok_f[pl.ds(j, 1), :])
        lanes = lax.broadcasted_iota(jnp.int32, (128, 128), 1).astype(jnp.float32)
        picked = None
        for t in range(4):
            cols = slice(128 * t, 128 * t + 128)
            p = jnp.where(tok == lanes + 128.0 * t, acc_t[0, rows, cols] - acc_d[0, rows, cols], 0.0)
            picked = p if picked is None else picked + p
        near[1, 8, pl.ds(4 + j, 1), :] = jnp.sum(picked.T, axis=0, keepdims=True)
        return carry

    lax.fori_loop(0, 4, pick, 0)
    lse = merge(gathered(*near_all(0)))
    spread(far, fs, fr, 0, far_me, 16, lse, far_to)
    lse = merge(gathered(*far_all(0)))
    near[0, 8] = lse
    tops[...] = jnp.exp(tops[...] - lse)

    def mass(j, carry):
        rows = pl.ds(pl.multiple_of(j * 128, 128), 128)
        t_col = columns(tops[pl.ds(j, 1), :])
        d_col = columns(tops[pl.ds(4 + j, 1), :])
        kept = None
        for t in range(4):
            cols = slice(128 * t, 128 * t + 128)
            e = jnp.maximum(part_t[rows, cols] * t_col - part_d[rows, cols] * d_col, 0.0)
            ex_ref[rows, cols] = e
            kept = e if kept is None else kept + e
        near[1, 8, pl.ds(j, 1), :] = jnp.sum(kept.T, axis=0, keepdims=True)
        return carry

    lax.fori_loop(0, 4, mass, 0)

    spread(near, ns, nr, 1, near_me, 8, near[1, 8], near_to)

    def normalize(j, carry):
        rows = pl.ds(pl.multiple_of(j * 128, 128), 128)
        t_col = columns(near[0, 8, pl.ds(j, 1), :])
        d_col = columns(near[0, 8, pl.ds(4 + j, 1), :])
        for t in range(4):
            cols = slice(128 * t, 128 * t + 128)
            lt_ref[rows, cols] = acc_t[0, rows, cols] - t_col
            ld_ref[rows, cols] = acc_d[0, rows, cols] - d_col
        return carry

    lax.fori_loop(0, 4, normalize, 0)
    for u in range(n_units):
        sent(u)
    for s in swaps + lent + sends:
        s.wait_send()
    others(*near_all(0)).wait_send()
    others(*far_all(0)).wait_send()
    both = jnp.sum(gathered(*near_all(1)), axis=0)
    spread(far, fs, fr, 1, far_me, 16, both, far_to)
    both = jnp.sum(gathered(*far_all(1)), axis=0)
    stat_ref[0:4, :] = both[0:4]
    stat_ref[4:8, :] = both[4:8] - (lse[0:4] - lse[4:8])

    others(*near_all(1)).wait_send()
    others(*far_all(1)).wait_send()


def finish(lt_ref, ld_ref, ex_ref, stat_ref, t_ref, d_ref, r_ref, accept_ref, left_ref, res, sem):
    copies = [pltpu.make_async_copy(lt_ref, t_ref, sem.at[0]), pltpu.make_async_copy(ld_ref, d_ref, sem.at[1])]
    for copy in copies:
        copy.start()
    left = stat_ref[0:4, :]
    left_ref[...] = left
    accept_ref[...] = jnp.exp(jnp.minimum(stat_ref[4:8, :], 0.0))
    scale = 1.0 / jnp.maximum(left, 0.25)
    for j in range(4):
        rows = slice(128 * j, 128 * j + 128)
        col = jnp.broadcast_to(scale[j : j + 1], (128, 128)).T
        for t in range(4):
            cols = slice(128 * t, 128 * t + 128)
            res[rows, cols] = ex_ref[rows, cols] * col
        copies.append(pltpu.make_async_copy(res.at[rows], r_ref.at[rows], sem.at[2 + j]))
        copies[-1].start()
    for copy in copies:
        copy.wait()


def on_device(target_hidden, target_weight, draft_hidden, draft_weight, draft_tokens):
    vmem, anywhere = pl.BlockSpec(memory_space=pltpu.VMEM), pl.BlockSpec(memory_space=pl.ANY)
    n_units = len(UNITS)
    dma = pltpu.SemaphoreType.DMA
    f32 = jnp.float32
    lt, ld, ex, stat = pl.pallas_call(
        kernel,
        name="verify",
        out_shape=(
            pltpu.VMEM((512, 512), f32),
            pltpu.VMEM((512, 512), f32),
            pltpu.VMEM((512, 512), f32),
            pltpu.VMEM((8, 128), f32),
        ),
        in_specs=[anywhere] * 5,
        out_specs=(vmem, vmem, vmem, vmem),
        scratch_shapes=(
            [pltpu.VMEM((2, 4, 4, 2, 16, size), jnp.bfloat16) for _, _, _, size in UNITS]
            + [pltpu.VMEM((2, 2, size, 512), jnp.bfloat16) for _, _, _, size in UNITS]
            + [
                pltpu.VMEM((4, 16384), jnp.bfloat16),
                pltpu.VMEM((4, 4096), jnp.bfloat16),
                pltpu.VMEM((4, 4, 4096), jnp.bfloat16),
                pltpu.VMEM((4, 4, 1024), jnp.bfloat16),
                pltpu.VMEM((2, 512, 512), f32),
                pltpu.VMEM((2, 512, 512), f32),
                pltpu.VMEM((512, 512), f32),
                pltpu.VMEM((512, 512), f32),
                pltpu.VMEM((4, 128), jnp.int32),
                pltpu.VMEM((4, 128), f32),
                pltpu.VMEM((8, 128), f32),
                pltpu.VMEM((2, 9, 8, 128), f32),
                pltpu.VMEM((2, 16, 8, 128), f32),
                dma((n_units,)), dma((n_units, 5)),
                dma((n_units,)), dma((n_units,)),
                dma((2, 4)), dma((2, 4)), dma((3,)),
                dma((2, 4)), dma((2, 4)),
                dma((2,)), dma((2,)),
                dma((2,)), dma((2,)),
            ]
        ),
        compiler_params=pltpu.CompilerParams(
            collective_id=0, has_side_effects=True, vmem_limit_bytes=48 * 2**20
        ),
    )(*[
        pltpu.with_memory_space_constraint(a, pltpu.HBM)
        for a in (
            target_hidden,
            target_weight.reshape(2, 2, 4096, 512),
            draft_hidden,
            draft_weight.reshape(2, 2, 1024, 512),
            draft_tokens.reshape(4, 128),
        )
    ])
    whole = jax.ShapeDtypeStruct((512, 512), f32)
    small = jax.ShapeDtypeStruct((4, 128), f32)
    held = [pltpu.with_memory_space_constraint(a, pltpu.VMEM) for a in (lt, ld, ex, stat)]
    t_log, d_log, residual, acceptance, leftover = pl.pallas_call(
        finish,
        name="finish",
        out_shape=(whole, whole, whole, small, small),
        in_specs=[vmem] * 4,
        out_specs=(anywhere, anywhere, anywhere, vmem, vmem),
        scratch_shapes=[pltpu.VMEM((512, 512), f32), dma((6,))],
        compiler_params=pltpu.CompilerParams(vmem_limit_bytes=8 * 2**20),
    )(*held)
    return t_log, d_log, residual, acceptance.reshape(512), leftover.reshape(512)


def solution(mesh):
    placed = (
        P(("wide", "narrow"), None),
        P(None, ("wide", "narrow")),
        P(("wide", "narrow"), None),
        P(None, ("wide", "narrow")),
        P(),
    )
    return jax.shard_map(
        on_device,
        mesh=mesh,
        in_specs=placed,
        out_specs=(
            P(None, ("wide", "narrow")),
            P(None, ("wide", "narrow")),
            P(None, ("wide", "narrow")),
            P(),
            P(),
        ),
        check_vma=False,
    )
```
